32 devices in a mesh: dp: 4 (over y, x), seq: 8 (over z, core).
Axes of the slice: x: 2, y: 2, z: 4, core: 2. Of those that a mesh axis runs over, the one named last changes fastest.
Arguments:
- inputs: bfloat16 [1024, 8, 1024], P('seq', 'dp'), may hold values from -6 to 6
- w_qkv: bfloat16 [1024, 3072], P('dp', 'seq'), may hold values from -0.1875 to 0.1875
- b_qkv: bfloat16 [3072], P(('seq', 'dp')), may hold values from -1 to 1
- w_out: bfloat16 [1024, 1024], P('seq', 'dp'), may hold values from -1.5 to 1.5
- b_out: bfloat16 [1024], P(('dp', 'seq')), may hold values from -1 to 1
- w_up: bfloat16 [1024, 4096], P('dp', 'seq'), may hold values from -0.1875 to 0.1875
- b_up: bfloat16 [4096], P(('seq', 'dp')), may hold values from -2 to 2
- w_down: bfloat16 [4096, 1024], P('seq', 'dp'), may hold values from -0.09375 to 0.09375
- b_down: bfloat16 [1024], P(('dp', 'seq')), may hold values from -1 to 1
- norm1_gain: bfloat16 [1024], P(('dp', 'seq')), may hold values from 0.5 to 1.5
- norm1_shift: bfloat16 [1024], P(('dp', 'seq')), may hold values from -1 to 1
- norm2_gain: bfloat16 [1024], P(('dp', 'seq')), may hold values from 0.5 to 1.5
- norm2_shift: bfloat16 [1024], P(('dp', 'seq')), may hold values from -1 to 1
- cotangent: bfloat16 [1024, 8, 1024], P('seq', 'dp'), may hold values from -6 to 6
Outputs:
- output: bfloat16 [1024, 8, 1024], P('seq', 'dp')
- grad_inputs: bfloat16 [1024, 8, 1024], P('seq', 'dp')
- grad_w_qkv: float32 [1024, 3072], P('dp', 'seq')
- grad_b_qkv: float32 [3072], P(('seq', 'dp'))
- grad_w_out: float32 [1024, 1024], P('seq', 'dp')
- grad_b_out: float32 [1024], P(('dp', 'seq'))
- grad_w_up: float32 [1024, 4096], P('dp', 'seq')
- grad_b_up: float32 [4096], P(('seq', 'dp'))
- grad_w_down: float32 [4096, 1024], P('seq', 'dp')
- grad_b_down: float32 [1024], P(('dp', 'seq'))
- grad_norm1_gain: float32 [1024], P(('dp', 'seq'))
- grad_norm1_shift: float32 [1024], P(('dp', 'seq'))
- grad_norm2_gain: float32 [1024], P(('dp', 'seq'))
- grad_norm2_shift: float32 [1024], P(('dp', 'seq'))
The draws below stay inside these ranges and needn't reach their ends.
All inputs are finite; a program needn't handle non-finite values.
Results may differ from the reference program's by a relative error of at most 0.011.
Values may be sent and summed in bfloat16 or wider, within the bound.
No kernel may reach another device: no remote copies, remote signals or barrier semaphores. Data moves between devices by JAX's collectives and lax.ppermute only.
A program may use at most 192 MiB of HBM per device.

```python
import math
import jax
import jax.numpy as jnp
from jax import lax

D = 1024
HEADS = 16
HEAD_DIM = 64
FF = 4096
ROTARY = 16
LEN = 1024
BATCH = 8


def block_scale(own_key, extent, pieces, low, high):
    level, own = 1.0, jax.random.fold_in(own_key, 6)
    for axis_at, blocks in pieces:
        draws = jnp.exp(jax.random.uniform(jax.random.fold_in(own, axis_at), (blocks,), jnp.float32, low / len(pieces), high / len(pieces)))
        level = level * jnp.repeat(draws, extent[axis_at] // blocks).reshape([-1 if axis == axis_at else 1 for axis in range(len(extent))])
    return level


def bell_draw(key, extent, scale, most, pieces=(), kind=jnp.bfloat16):
    entries = scale * jax.random.normal(key, extent, jnp.float32)
    if pieces:
        entries = entries * block_scale(key, extent, pieces, -0.22, 0.18)
    return jnp.clip(entries, -most, most).astype(kind)


def setup_inputs(seed: int = 0) -> dict:
    key_of = jax.random.split(jax.random.key(seed), 15)
    inputs = bell_draw(key_of[0], (LEN, BATCH, D), 1.0, 6.0, ((0, 8), (1, 4)))
    w_qkv = bell_draw(key_of[1], (D, 3 * D), D ** -0.5, 0.1875, ((0, 4), (1, 8)))
    b_qkv = bell_draw(key_of[2], (3 * D,), 0.2, 1.0, ((0, 32),))
    w_out = bell_draw(key_of[3], (D, D), 16 ** -0.5, 1.5, ((0, 8), (1, 4)))
    b_out = bell_draw(key_of[4], (D,), 0.2, 1.0, ((0, 32),))
    w_up = bell_draw(key_of[5], (D, FF), D ** -0.5, 0.1875, ((0, 4), (1, 8)))
    b_up = bell_draw(key_of[6], (FF,), 0.5, 2.0, ((0, 32),))
    w_down = bell_draw(key_of[7], (FF, D), FF ** -0.5, 0.09375, ((0, 8), (1, 4)))
    b_down = bell_draw(key_of[8], (D,), 0.2, 1.0, ((0, 32),))
    norm1_gain = jnp.clip(1.0 + 0.1 * jax.random.normal(key_of[9], (D,), jnp.float32), 0.5, 1.5).astype(jnp.bfloat16)
    norm1_shift = bell_draw(key_of[10], (D,), 0.2, 1.0, ((0, 32),))
    norm2_gain = jnp.clip(1.0 + 0.1 * jax.random.normal(key_of[11], (D,), jnp.float32), 0.5, 1.5).astype(jnp.bfloat16)
    norm2_shift = bell_draw(key_of[12], (D,), 0.2, 1.0, ((0, 32),))
    cotangent = bell_draw(key_of[13], (LEN, BATCH, D), 1.0, 6.0, ((0, 8), (1, 4)))
    return {"inputs": inputs, "w_qkv": w_qkv, "b_qkv": b_qkv, "w_out": w_out, "b_out": b_out, "w_up": w_up, "b_up": b_up, "w_down": w_down, "b_down": b_down, "norm1_gain": norm1_gain, "norm1_shift": norm1_shift, "norm2_gain": norm2_gain, "norm2_shift": norm2_shift, "cotangent": cotangent}


EPSILON = 1e-05
NEGATIVE = -1e+30

def rounded(values):
    return lax.optimization_barrier(values.astype(jnp.bfloat16)).astype(jnp.float32)

def widened(values):
    return values.astype(jnp.float32)

def normalize(values, gain, shift):
    mean_value = lax.optimization_barrier(jnp.mean(values, axis=-1, keepdims=True))
    centred = values - mean_value
    variance = lax.optimization_barrier(jnp.mean(centred * centred, axis=-1, keepdims=True))
    inverse = lax.rsqrt(variance + EPSILON)
    scaled = centred * inverse
    return (scaled * gain + shift, scaled, inverse)

def normalize_back(grad_hidden, scaled, inverse, gain):
    grad_scaled = grad_hidden * gain
    centre = lax.optimization_barrier(jnp.mean(grad_scaled, axis=-1, keepdims=True))
    along = lax.optimization_barrier(jnp.mean(grad_scaled * scaled, axis=-1, keepdims=True))
    grad_source = inverse * (grad_scaled - centre - scaled * along)
    width = grad_hidden.shape[-1]
    gain_sum = lax.optimization_barrier(jnp.sum((grad_hidden * scaled).reshape(-1, width), 0))
    shift_sum = lax.optimization_barrier(jnp.sum(grad_hidden.reshape(-1, width), 0))
    return (grad_source, gain_sum, shift_sum)

def rotary_tables(positions, rotary):
    half = rotary // 2
    freqs = 10000.0 ** (-jnp.arange(half, dtype=jnp.float32) * 2.0 / rotary)
    angles = positions[:, None] * freqs[None, :]
    cosine = jnp.cos(angles)
    sine = jnp.sin(angles)
    return (jnp.concatenate([cosine, cosine], 1), jnp.concatenate([sine, sine], 1))

def rotate(values, cosine, sine):
    rotary = cosine.shape[-1]
    half = rotary // 2
    front = values[..., :rotary]
    turned = jnp.concatenate([-front[..., half:], front[..., :half]], -1)
    moved = front * cosine + turned * sine
    return jnp.concatenate([moved, values[..., rotary:]], -1)

def gelu_value(values):
    return 0.5 * values * (1.0 + lax.erf(values * 0.7071067811865476))

def gelu_slope(values):
    return 0.5 * (1.0 + lax.erf(values * 0.7071067811865476)) + values * 0.3989422804014327 * jnp.exp(-0.5 * values * values)

def reference(inputs, w_qkv, b_qkv, w_out, b_out, w_up, b_up, w_down, b_down, norm1_gain, norm1_shift, norm2_gain, norm2_shift, cotangent):
    wide_type = jnp.float32
    half_type = jnp.bfloat16
    scale_factor = HEAD_DIM ** (-0.5)
    block = math.gcd(LEN, 512)
    count = LEN // block
    positions = jnp.arange(LEN, dtype=jnp.int32)
    cosine, sine = rotary_tables(positions.astype(wide_type), ROTARY)
    cos_rows = cosine[:, None, :]
    sin_rows = sine[:, None, :]
    contract_rows = (((0,), (0,)), ((), ()))
    contract_cols = (((1,), (1,)), ((), ()))

    def one_sequence(totals, pair):
        source_b, grad_b = pair
        source = widened(source_b)
        normed_one, scaled_one, inverse_one = normalize(source, widened(norm1_gain), widened(norm1_shift))
        normed_two, scaled_two, inverse_two = normalize(source, widened(norm2_gain), widened(norm2_shift))
        hidden_one = normed_one.astype(half_type)
        hidden_two = normed_two.astype(half_type)
        projected = jnp.dot(hidden_one, w_qkv, preferred_element_type=wide_type) + widened(b_qkv)
        projected = projected.reshape(LEN, HEADS, 3, HEAD_DIM)
        query = rotate(projected[:, :, 0], cos_rows, sin_rows).astype(half_type)
        keys = rotate(projected[:, :, 1], cos_rows, sin_rows).astype(half_type)
        values = projected[:, :, 2].astype(half_type)
        key_wide = widened(keys)
        value_wide = widened(values)

        def masked_scores(query_block, start):
            allowed = positions[None, :] <= (start + jnp.arange(block, dtype=jnp.int32))[:, None]
            scores = jnp.einsum('qhd,khd->hqk', query_block, key_wide) * scale_factor
            return (jnp.where(allowed[None], scores, NEGATIVE), allowed)

        def forward_block(index):
            start = index * block
            query_block = widened(lax.dynamic_slice_in_dim(query, start, block, 0))
            scores, allowed = masked_scores(query_block, start)
            peak = lax.optimization_barrier(jnp.max(scores, -1))
            weights = jnp.where(allowed[None], jnp.exp(scores - peak[..., None]), 0.0)
            total = lax.optimization_barrier(jnp.sum(weights, -1))
            mixed = jnp.einsum('hqk,khd->qhd', rounded(weights), value_wide) / total.T[:, :, None]
            return (mixed, peak + jnp.log(total))
        attended, log_total = lax.map(forward_block, jnp.arange(count, dtype=jnp.int32))
        attended = attended.reshape(LEN, HEADS, HEAD_DIM)
        log_total = jnp.transpose(log_total, (1, 0, 2)).reshape(HEADS, LEN)
        attended_b = attended.reshape(LEN, D).astype(half_type)
        attention_out = jnp.dot(attended_b, w_out, preferred_element_type=wide_type) + widened(b_out)
        up_pre = jnp.dot(hidden_two, w_up, preferred_element_type=wide_type) + widened(b_up)
        activated = gelu_value(up_pre).astype(half_type)
        mlp_out = jnp.dot(activated, w_down, preferred_element_type=wide_type) + widened(b_down)
        output = (source + attention_out + mlp_out).astype(half_type)
        grad_f = widened(grad_b)
        grad_attended = lax.dot_general(grad_b, w_out, contract_cols, preferred_element_type=wide_type).reshape(LEN, HEADS, HEAD_DIM)
        delta = lax.optimization_barrier(jnp.sum(grad_attended * attended, -1)).T
        grad_attended_b = grad_attended.astype(half_type)

        def backward_block(carry, index):
            grad_keys, grad_values = carry
            start = index * block
            query_block = widened(lax.dynamic_slice_in_dim(query, start, block, 0))
            grad_block = widened(lax.dynamic_slice_in_dim(grad_attended_b, start, block, 0))
            delta_block = lax.dynamic_slice_in_dim(delta, start, block, 1)
            total_block = lax.dynamic_slice_in_dim(log_total, start, block, 1)
            scores, allowed = masked_scores(query_block, start)
            probs = jnp.where(allowed[None], jnp.exp(scores - total_block[..., None]), 0.0)
            grad_probs = jnp.einsum('qhd,khd->hqk', grad_block, value_wide)
            grad_scores = rounded(probs * (grad_probs - delta_block[..., None]))
            grad_query = jnp.einsum('hqk,khd->qhd', grad_scores, key_wide) * scale_factor
            grad_keys = grad_keys + jnp.einsum('hqk,qhd->khd', grad_scores, query_block) * scale_factor
            grad_values = grad_values + jnp.einsum('hqk,qhd->khd', rounded(probs), grad_block)
            return ((grad_keys, grad_values), grad_query)
        empty = jnp.zeros((LEN, HEADS, HEAD_DIM), wide_type)
        (grad_keys, grad_values), grad_query = lax.scan(backward_block, (empty, empty), jnp.arange(count, dtype=jnp.int32))
        grad_query = grad_query.reshape(LEN, HEADS, HEAD_DIM)
        grad_query_in = rotate(grad_query, cos_rows, -sin_rows)
        grad_keys_in = rotate(grad_keys, cos_rows, -sin_rows)
        grad_projected = jnp.stack([grad_query_in, grad_keys_in, grad_values], 2).reshape(LEN, 3 * D)
        grad_projected_b = grad_projected.astype(half_type)
        grad_hidden_one = lax.dot_general(grad_projected_b, w_qkv, contract_cols, preferred_element_type=wide_type)
        grad_gelu = lax.dot_general(grad_b, w_down, contract_cols, preferred_element_type=wide_type)
        grad_up = grad_gelu * gelu_slope(up_pre)
        grad_up_b = grad_up.astype(half_type)
        grad_hidden_two = lax.dot_general(grad_up_b, w_up, contract_cols, preferred_element_type=wide_type)
        grad_source_one, gain_one, shift_one = normalize_back(grad_hidden_one, scaled_one, inverse_one, widened(norm1_gain))
        grad_source_two, gain_two, shift_two = normalize_back(grad_hidden_two, scaled_two, inverse_two, widened(norm2_gain))
        grad_inputs = (grad_f + grad_source_one + grad_source_two).astype(half_type)
        bias_sum = lax.optimization_barrier(jnp.sum(grad_f, 0))
        terms = (lax.dot_general(hidden_one, grad_projected_b, contract_rows, preferred_element_type=wide_type), lax.optimization_barrier(jnp.sum(grad_projected, 0)), lax.dot_general(attended_b, grad_b, contract_rows, preferred_element_type=wide_type), bias_sum, lax.dot_general(hidden_two, grad_up_b, contract_rows, preferred_element_type=wide_type), lax.optimization_barrier(jnp.sum(grad_up, 0)), lax.dot_general(activated, grad_b, contract_rows, preferred_element_type=wide_type), bias_sum, gain_one, shift_one, gain_two, shift_two)
        totals = tuple((first + second for first, second in zip(totals, terms)))
        return (totals, (output, grad_inputs))
    start_totals = (jnp.zeros((D, 3 * D), wide_type), jnp.zeros((3 * D,), wide_type), jnp.zeros((D, D), wide_type), jnp.zeros((D,), wide_type), jnp.zeros((D, FF), wide_type), jnp.zeros((FF,), wide_type), jnp.zeros((FF, D), wide_type), jnp.zeros((D,), wide_type), jnp.zeros((D,), wide_type), jnp.zeros((D,), wide_type), jnp.zeros((D,), wide_type), jnp.zeros((D,), wide_type))
    sequences = jnp.swapaxes(inputs, 0, 1)
    grads_in = jnp.swapaxes(cotangent, 0, 1)
    totals, (outputs, grad_inputs) = lax.scan(one_sequence, start_totals, (sequences, grads_in))
    outputs = jnp.swapaxes(outputs, 0, 1)
    grad_inputs = jnp.swapaxes(grad_inputs, 0, 1)
    return (outputs, grad_inputs, totals[0], totals[1], totals[2], totals[3], totals[4], totals[5], totals[6], totals[7], totals[8], totals[9], totals[10], totals[11])
```

```python
import functools
import math

import jax
import jax.numpy as jnp
from jax import lax
from jax.experimental import pallas as pl
from jax.experimental.pallas import tpu as pltpu
from jax.sharding import PartitionSpec as P

HEAD_DIM = 64
ROTARY = 16
EPSILON = 1e-05
NEGATIVE = -1e30
F32 = jnp.float32
BF16 = jnp.bfloat16
VMEM_LIMIT = 50 * 1024 * 1024


def dot_nn(a, b):
    return lax.dot_general(a, b, (((1,), (0,)), ((), ())), preferred_element_type=F32)


def dot_nt(a, b):
    return lax.dot_general(a, b, (((1,), (1,)), ((), ())), preferred_element_type=F32)


def dot_tn(a, b):
    return lax.dot_general(a, b, (((0,), (0,)), ((), ())), preferred_element_type=F32)


def flip(value, axis, size, bit):
    return lax.ppermute(value, axis, [(i, i ^ (1 << bit)) for i in range(size)])


def cube_gather(value, axis, size, bits):
    index = lax.axis_index(axis)
    done = []
    for bit in bits:
        other = flip(value, axis, size, bit)
        mine = (index >> bit) & 1
        low = jnp.where(mine == 0, value, other)
        high = jnp.where(mine == 0, other, value)
        place = sum(1 for b in done if b > bit)
        value = jnp.stack([low, high], axis=place)
        done.append(bit)
    return value.reshape((size,) + value.shape[len(done) :])


def cube_reduce(value, axis, size, bits):
    index = lax.axis_index(axis)
    left = list(range(len(bits)))[::-1]
    value = value.reshape((2,) * len(bits) + value.shape[1:])
    for bit in bits:
        place = left.index(bit)
        mine = (index >> bit) & 1
        sent = lax.dynamic_index_in_dim(value, 1 - mine, place, keepdims=False)
        kept = lax.dynamic_index_in_dim(value, mine, place, keepdims=False)
        got = flip(sent, axis, size, bit)
        value = (kept.astype(F32) + got.astype(F32)).astype(value.dtype)
        left.remove(bit)
    return value


def ring(value, size):
    return lax.ppermute(value, "seq", [(i, (i + 2) % size) for i in range(size)])


def swap(value, size):
    return lax.ppermute(value, "seq", [(i, i ^ 1) for i in range(size)])


def ring_gather(value, size):
    own, other = [value], [swap(value, size)]
    for _ in range(size // 2 - 1):
        value = ring(value, size)
        own.append(value)
        other.append(swap(value, size))
    return own + other


def ring_scatter(parts, size):
    chips = size // 2
    rows = parts.shape[0] // size
    got = swap(parts[chips * rows :], size)

    def own(step):
        at = ((step + 1) % chips) * rows
        return parts[at : at + rows].astype(F32) + got[at : at + rows].astype(F32)

    total = own(0)
    for step in range(1, chips):
        total = ring(total.astype(BF16), size).astype(F32) + own(step)
    return total


def turn(values, cosine, first, second):
    parts = []
    for at in range(0, values.shape[1], 128):
        part = values[:, at : at + 128]
        parts.append(
            part * cosine
            + pltpu.roll(part, 120, 1) * first
            + pltpu.roll(part, 8, 1) * second
        )
    return parts[0] if len(parts) == 1 else jnp.concatenate(parts, 1)


def head_stack(rows, heads):
    if heads == 1:
        return rows
    lane = lax.broadcasted_iota(jnp.int32, rows.shape, 1) // HEAD_DIM
    return jnp.concatenate(
        [jnp.where(lane == head, rows, jnp.zeros_like(rows)) for head in range(heads)], 0
    )


def head_rows(rows, heads, columns):
    if heads == 1:
        return rows
    return jnp.concatenate([rows[h : h + 1, columns] for h in range(heads)], 1)


def table_rows(ref, perm_ref, first, count, unit):
    parts = [
        ref[pl.ds(pl.multiple_of(perm_ref[first + n] * unit, unit), unit), :] for n in range(count)
    ]
    return jnp.concatenate(parts, 0)


def forward_kernel(
    heads,
    unit,
    group,
    block,
    perm_ref,
    x_ref,
    w_ref,
    bias_ref,
    cos_ref,
    first_ref,
    second_ref,
    wo_ref,
    wd_ref,
    scaled_ref,
    act_ref,
    slope_ref,
    q_ref,
    k_ref,
    v_ref,
    att_ref,
    lse_ref,
    attb_ref,
    out_ref,
    att_rows,
):
    length = x_ref.shape[0]
    g = heads * HEAD_DIM
    count = group // unit

    def project(step, carry):
        at = pl.multiple_of(step * group, group)
        rows = pl.ds(at, group)
        x = x_ref[rows, :].astype(F32)
        mean = jnp.mean(x, axis=1, keepdims=True)
        centred = x - mean
        variance = jnp.mean(centred * centred, axis=1, keepdims=True)
        scaled = (centred * lax.rsqrt(variance + EPSILON)).astype(BF16)
        scaled_ref[rows, :] = scaled
        made = dot_nn(scaled, w_ref[...]) + bias_ref[...]
        first = step * count
        cosine = table_rows(cos_ref, perm_ref, first, count, unit)
        one = table_rows(first_ref, perm_ref, first, count, unit)
        two = table_rows(second_ref, perm_ref, first, count, unit)
        turned = turn(made[:, : 2 * g], cosine, one, two)
        query = (turned[:, :g] * (HEAD_DIM**-0.5)).astype(BF16)
        keys = turned[:, g:].astype(BF16)
        values = made[:, 2 * g : 3 * g].astype(BF16)
        for n in range(count):
            to = pl.ds(pl.multiple_of(perm_ref[first + n] * unit, unit), unit)
            q_ref[to, :] = query[n * unit : (n + 1) * unit]
            k_ref[to, :] = keys[n * unit : (n + 1) * unit]
            v_ref[to, :] = values[n * unit : (n + 1) * unit]
        up = made[:, 3 * g :]
        phi = 0.5 * (1.0 + lax.erf(up * 0.7071067811865476))
        act_ref[rows, :] = (up * phi).astype(BF16)
        slope_ref[rows, :] = (
            phi + up * 0.3989422804014327 * jnp.exp(-0.5 * up * up)
        ).astype(BF16)
        return carry

    lax.fori_loop(0, length // group, project, 0)

    turned_v = v_ref[...].astype(F32).T.astype(BF16)
    key_at = lax.broadcasted_iota(jnp.int32, (block, heads * block), 0)
    query_at = lax.broadcasted_iota(jnp.int32, (block, heads * block), 1) % block
    allowed = key_at <= query_at
    for i in range(length // block):
        here = slice(i * block, (i + 1) * block)
        stack = head_stack(q_ref[here, :], heads)
        scores = [dot_nt(k_ref[n * block : (n + 1) * block, :], stack) for n in range(i + 1)]
        scores[i] = jnp.where(allowed, scores[i], NEGATIVE)
        peak = jnp.max(scores[0], axis=0, keepdims=True)
        for n in range(1, i + 1):
            peak = jnp.maximum(peak, jnp.max(scores[n], axis=0, keepdims=True))
        total = jnp.zeros_like(peak)
        mixed = jnp.zeros((g, heads * block), F32)
        for n in range(i + 1):
            weights = jnp.exp(scores[n] - peak)
            total = total + jnp.sum(weights, axis=0, keepdims=True)
            mixed = mixed + dot_nn(
                turned_v[:, n * block : (n + 1) * block], weights.astype(BF16)
            )
        mixed = mixed / total
        log_total = peak + jnp.log(total)
        parts = []
        for h in range(heads):
            span = slice(h * block, (h + 1) * block)
            parts.append(mixed[h * HEAD_DIM : (h + 1) * HEAD_DIM, span])
            lse_ref[h : h + 1, here] = log_total[:, span]
        attended = parts[0] if heads == 1 else jnp.concatenate(parts, 0)
        att_ref[:, here] = attended
        att_rows[here, :] = attended.T

    def finish(step, carry):
        rows = pl.ds(pl.multiple_of(step * group, group), group)
        attended = table_rows(att_rows, perm_ref, step * count, count, unit).astype(BF16)
        attb_ref[rows, :] = attended
        out_ref[rows, :] = (
            dot_nn(attended, wo_ref[...]) + dot_nn(act_ref[rows, :], wd_ref[...])
        ).astype(BF16)
        return carry

    lax.fori_loop(0, length // group, finish, 0)


def backward_kernel(
    heads,
    unit,
    group,
    block,
    perm_ref,
    grad_ref,
    wot_ref,
    wt_ref,
    cos_ref,
    first_ref,
    second_ref,
    q_ref,
    k_ref,
    v_ref,
    att_ref,
    lse_ref,
    gup_ref,
    gp_ref,
    sums_ref,
    e_ref,
    ga_rows,
    dq_rows,
    dk_rows,
    dv_rows,
):
    length = grad_ref.shape[0]
    g = heads * HEAD_DIM
    count = group // unit

    def attend(step, carry):
        rows = pl.ds(pl.multiple_of(step * group, group), group)
        made = dot_nn(grad_ref[rows, :], wot_ref[...])
        for n in range(count):
            to = pl.ds(pl.multiple_of(perm_ref[step * count + n] * unit, unit), unit)
            ga_rows[to, :] = made[n * unit : (n + 1) * unit]
        return carry

    lax.fori_loop(0, length // group, attend, 0)

    turned_k = k_ref[...].astype(F32).T.astype(BF16)
    key_at = lax.broadcasted_iota(jnp.int32, (block, heads * block), 0)
    query_at = lax.broadcasted_iota(jnp.int32, (block, heads * block), 1) % block
    allowed = key_at <= query_at
    for i in range(length // block):
        here = slice(i * block, (i + 1) * block)
        queries = head_stack(q_ref[here, :], heads)
        grad = ga_rows[here, :]
        grads = head_stack(grad.astype(BF16), heads)
        product = grad.T * att_ref[:, here]
        delta = [
            jnp.sum(product[h * HEAD_DIM : (h + 1) * HEAD_DIM], axis=0, keepdims=True)
            for h in range(heads)
        ]
        delta = delta[0] if heads == 1 else jnp.concatenate(delta, 1)
        log_total = [lse_ref[h : h + 1, here] for h in range(heads)]
        log_total = log_total[0] if heads == 1 else jnp.concatenate(log_total, 1)
        turned_q = [jnp.zeros((HEAD_DIM, block), F32) for _ in range(heads)]
        for n in range(i + 1):
            there = slice(n * block, (n + 1) * block)
            probs = jnp.exp(dot_nt(k_ref[there, :], queries) - log_total)
            if n == i:
                probs = jnp.where(allowed, probs, 0.0)
            grad_scores = (probs * (dot_nt(v_ref[there, :], grads) - delta)).astype(BF16)
            value_part = dot_nn(probs.astype(BF16), grads)
            key_part = dot_nn(grad_scores, queries)
            if n == i:
                dv_rows[there, :] = value_part
                dk_rows[there, :] = key_part
            else:
                dv_rows[there, :] += value_part
                dk_rows[there, :] += key_part
            for h in range(heads):
                turned_q[h] = turned_q[h] + dot_nn(
                    turned_k[h * HEAD_DIM : (h + 1) * HEAD_DIM, there],
                    grad_scores[:, h * block : (h + 1) * block],
                )
        whole = turned_q[0] if heads == 1 else jnp.concatenate(turned_q, 0)
        dq_rows[here, :] = whole.T * (HEAD_DIM**-0.5)

    sums_ref[...] = jnp.zeros_like(sums_ref)

    def finish(step, carry):
        rows = pl.ds(pl.multiple_of(step * group, group), group)
        first = step * count
        cosine = table_rows(cos_ref, perm_ref, first, count, unit)
        one = table_rows(first_ref, perm_ref, first, count, unit)
        two = table_rows(second_ref, perm_ref, first, count, unit)
        both = jnp.concatenate(
            [
                table_rows(dq_rows, perm_ref, first, count, unit),
                table_rows(dk_rows, perm_ref, first, count, unit),
            ],
            1,
        )
        both = turn(both, cosine, -one, -two)
        values = table_rows(dv_rows, perm_ref, first, count, unit)
        made = jnp.concatenate([both, values], 1)
        sums_ref[0:1, :] += jnp.sum(made, axis=0, keepdims=True)
        made = made.astype(BF16)
        gp_ref[rows, :] = made
        e_ref[rows, :] = (
            dot_nn(made, wt_ref[: 3 * g, :]) + dot_nn(gup_ref[rows, :], wt_ref[3 * g :, :])
        ).astype(BF16)
        return carry

    lax.fori_loop(0, length // group, finish, 0)


def kernel_call(body, outs, scratch, flops, args):
    specs = [pl.BlockSpec(memory_space=pltpu.SMEM)] + [
        pl.BlockSpec(memory_space=pltpu.VMEM) for _ in args[1:]
    ]
    size = sum(math.prod(a.shape) * a.dtype.itemsize for a in list(args) + list(outs))
    return pl.pallas_call(
        body,
        out_shape=tuple(outs),
        in_specs=specs,
        out_specs=tuple(pl.BlockSpec(memory_space=pltpu.VMEM) for _ in outs),
        scratch_shapes=scratch,
        compiler_params=pltpu.CompilerParams(vmem_limit_bytes=VMEM_LIMIT),
        cost_estimate=pl.CostEstimate(
            flops=int(flops), bytes_accessed=int(size), transcendentals=0
        ),
    )(*args)


def shaped(*shape, dtype=BF16):
    return jax.ShapeDtypeStruct(shape, dtype)


def rotary_tables(length):
    half = ROTARY // 2
    freqs = 10000.0 ** (-jnp.arange(half, dtype=F32) * 2.0 / ROTARY)
    angles = jnp.arange(length, dtype=jnp.int32).astype(F32)[:, None] * freqs[None, :]
    cosine, sine = jnp.cos(angles), jnp.sin(angles)
    none = jnp.zeros_like(sine)
    rest = jnp.zeros((length, HEAD_DIM - ROTARY), F32)
    cos_head = jnp.concatenate([cosine, cosine, rest + 1.0], 1)
    first = jnp.concatenate([-sine, none, rest], 1)
    second = jnp.concatenate([none, sine, rest], 1)
    return tuple(jnp.concatenate([t, t], 1) for t in (cos_head, first, second))


def split_heads(values, heads, back=False):
    lead = values.shape[:-1]
    shape = (3, heads, HEAD_DIM) if back else (heads, 3, HEAD_DIM)
    return jnp.swapaxes(values.reshape(lead + shape), -3, -2).reshape(values.shape)


def local(
    dp,
    seq,
    inputs,
    w_qkv,
    b_qkv,
    w_out,
    b_out,
    w_up,
    b_up,
    w_down,
    b_down,
    norm1_gain,
    norm1_shift,
    norm2_gain,
    norm2_shift,
    cotangent,
):
    span, count, width = inputs.shape
    length = span * seq
    chips = seq // 2
    qkv_cols = w_qkv.shape[1]
    heads = qkv_cols // (3 * HEAD_DIM)
    g = heads * HEAD_DIM
    dp_bits = list(range(dp.bit_length() - 1))
    seq_bits = list(range(seq.bit_length() - 1))
    me = lax.axis_index("seq")
    chip, core = me // 2, me % 2
    steps = jnp.arange(chips, dtype=jnp.int32)
    there = lax.rem(chip - steps + chips, chips) * 2
    perm = jnp.concatenate([there + core, there + 1 - core]).astype(jnp.int32)
    tables = rotary_tables(length)

    sources = [inputs[:, s] for s in range(count)]
    grads = [cotangent[:, s] for s in range(count)]

    norms = jnp.stack([norm1_gain, norm1_shift, norm2_gain, norm2_shift, b_out, b_down])
    small = jnp.concatenate([norms.reshape(-1), b_qkv, b_up])
    small = cube_gather(small, "dp", dp, dp_bits)
    in_block = jnp.concatenate([split_heads(w_qkv, heads), w_up], 1)
    out_block = jnp.concatenate([w_out, w_down], 0)
    w_in = cube_gather(in_block, "dp", dp, dp_bits).reshape(width, in_block.shape[1])
    w_back = cube_gather(out_block, "dp", dp, dp_bits[::-1])
    w_back = jnp.swapaxes(w_back, 0, 1).reshape(out_block.shape[0], width)
    norms = cube_gather(small[:, : norms.size], "seq", seq, seq_bits)
    norms = norms.reshape(seq, dp, 6, -1).transpose(2, 1, 0, 3).reshape(6, width).astype(F32)
    gain_one, shift_one, gain_two, shift_two, out_bias, down_bias = [norms[i] for i in range(6)]
    at = 6 * norm1_gain.size
    qkv_bias = split_heads(small[:, at : at + b_qkv.size].reshape(-1), heads)
    up_bias = small[:, at + b_qkv.size :].reshape(-1)

    gathered = [jnp.concatenate(ring_gather(s, seq), 0) for s in sources]
    grad_rows = [jnp.concatenate(ring_gather(s, seq), 0) for s in grads]

    wide = w_in.astype(F32)
    is_qkv = lax.broadcasted_iota(jnp.int32, (1, w_in.shape[1]), 1) < qkv_cols
    gains = jnp.where(is_qkv, gain_one[:, None], gain_two[:, None])
    shifts = jnp.where(is_qkv, shift_one[:, None], shift_two[:, None])
    folded = (wide * gains).astype(BF16)
    folded_t = folded.T
    bias = jnp.sum(wide * shifts, 0, keepdims=True) + jnp.concatenate(
        [qkv_bias, up_bias]
    ).astype(F32)[None]
    wo, wd = w_back[:g], w_back[g:]
    wo_t = wo.T
    hidden = wd.shape[0]

    unit = span
    group = math.gcd(length, 256)
    block = math.gcd(length, 256)
    matmul = 2.0 * length * width
    pairs = 2.0 * heads * length * length * 64

    forward = []
    for s in range(count):
        forward.append(
            kernel_call(
                functools.partial(forward_kernel, heads, unit, group, block),
                [
                    shaped(length, width),
                    shaped(length, hidden),
                    shaped(length, hidden),
                    shaped(length, g),
                    shaped(length, g),
                    shaped(length, g),
                    shaped(g, length, dtype=F32),
                    shaped(heads, length, dtype=F32),
                    shaped(length, g),
                    shaped(length, width),
                ],
                [pltpu.VMEM((length, g), F32)],
                matmul * (4 * g + 2 * hidden) + 8 * pairs,
                (perm, gathered[s], folded, bias, *tables, wo, wd),
            )
        )
    branches = [ring_scatter(f[9], seq) for f in forward]

    grad_up_rows, up_sums = [], 0.0
    for s in range(count):
        made = dot_nt(grad_rows[s], wd) * forward[s][2].astype(F32)
        up_sums = up_sums + jnp.sum(made, 0)
        grad_up_rows.append(made.astype(BF16))
    grad_back = sum(
        dot_tn(jnp.concatenate([forward[s][8], forward[s][1]], 1), grad_rows[s])
        for s in range(count)
    )
    grad_back = grad_back.astype(BF16).reshape(g + hidden, dp, -1)
    grad_back = cube_reduce(jnp.swapaxes(grad_back, 0, 1), "dp", dp, dp_bits)
    scaled_up = sum(dot_tn(forward[s][0], grad_up_rows[s]) for s in range(count))

    backward = []
    for s in range(count):
        f = forward[s]
        backward.append(
            kernel_call(
                functools.partial(backward_kernel, heads, unit, group, block),
                [
                    shaped(length, 3 * g),
                    shaped(8, 3 * g, dtype=F32),
                    shaped(length, width),
                ],
                [pltpu.VMEM((length, g), F32) for _ in range(4)],
                matmul * (4 * g + hidden) + 16 * pairs,
                (perm, grad_rows[s], wo_t, folded_t, *tables, *f[3:8], grad_up_rows[s]),
            )
        )
    pulled = [ring_scatter(b[2], seq) for b in backward]
    scaled_qkv = sum(dot_tn(forward[s][0], backward[s][0]) for s in range(count))
    qkv_sums = sum(b[1][0] for b in backward)

    def to_owner(part, gain, shift, sums):
        made = gain[:, None] * part + shift[:, None] * sums[None]
        made = made.astype(BF16).reshape(dp, width // dp, -1)
        return cube_reduce(made, "dp", dp, dp_bits[::-1]).astype(F32)

    grad_w_up = to_owner(scaled_up, gain_two, shift_two, up_sums)
    grad_w_qkv = to_owner(scaled_qkv, gain_one, shift_one, qkv_sums)
    grad_w_qkv = split_heads(grad_w_qkv, heads, back=True)
    grad_w_out, grad_w_down = grad_back[:g].astype(F32), grad_back[g:].astype(F32)

    w_one, w_two = wide[:, :qkv_cols], wide[:, qkv_cols:]
    bias_sum = sum(jnp.sum(g_s.astype(F32), 0) for g_s in grads)
    vectors = jnp.stack(
        [
            jnp.sum(w_one * scaled_qkv, 1),
            jnp.sum(w_one * qkv_sums[None], 1),
            jnp.sum(w_two * scaled_up, 1),
            jnp.sum(w_two * up_sums[None], 1),
            bias_sum,
        ]
    )
    vectors = vectors.reshape(5, dp, seq, -1).transpose(1, 2, 0, 3).reshape(dp, -1)
    biases = jnp.concatenate(
        [
            split_heads(qkv_sums, heads, back=True).reshape(dp, -1),
            up_sums.reshape(dp, -1),
        ],
        1,
    )
    summed = cube_reduce(jnp.concatenate([vectors, biases], 1), "dp", dp, dp_bits)
    cut = vectors.shape[1]
    grad_b_qkv = summed[cut : cut + b_qkv.size]
    grad_b_up = summed[cut + b_qkv.size :]
    norms_out = cube_reduce(summed[:cut].reshape(seq, 5, -1), "seq", seq, seq_bits)

    outputs, grads_in = [], []
    for s in range(count):
        source = sources[s].astype(F32)
        outputs.append((source + branches[s] + (out_bias + down_bias)[None]).astype(BF16))
        mean = jnp.mean(source, 1, keepdims=True)
        centred = source - mean
        inverse = lax.rsqrt(jnp.mean(centred * centred, 1, keepdims=True) + EPSILON)
        scaled = centred * inverse
        e = pulled[s]
        middle = jnp.mean(e, 1, keepdims=True)
        along = jnp.mean(e * scaled, 1, keepdims=True)
        grads_in.append(
            (grads[s].astype(F32) + inverse * (e - middle - scaled * along)).astype(BF16)
        )
    return (
        jnp.stack(outputs, 1),
        jnp.stack(grads_in, 1),
        grad_w_qkv,
        grad_b_qkv,
        grad_w_out,
        norms_out[4],
        grad_w_up,
        grad_b_up,
        grad_w_down,
        norms_out[4],
        norms_out[0],
        norms_out[1],
        norms_out[2],
        norms_out[3],
    )


def solution(mesh):
    tokens = P("seq", "dp", None)
    rows, columns = P("dp", "seq"), P("seq", "dp")
    wide, flat = P(("seq", "dp")), P(("dp", "seq"))
    return jax.shard_map(
        functools.partial(local, mesh.shape["dp"], mesh.shape["seq"]),
        mesh=mesh,
        in_specs=(
            tokens, rows, wide, columns, flat, rows, wide, columns, flat, flat, flat, flat, flat,
            tokens,
        ),
        out_specs=(
            tokens, tokens, rows, wide, columns, flat, rows, wide, columns, flat, flat, flat,
            flat, flat,
        ),
        check_vma=False,
    )
```

```python
import functools
import math

import jax
import jax.numpy as jnp
import numpy as np
from jax import lax
from jax.experimental import pallas as pl
from jax.experimental.pallas import tpu as pltpu
from jax.sharding import PartitionSpec as P

HEAD_DIM = 64
ROTARY = 16
EPSILON = 1e-05
NEGATIVE = -1e30
F32 = jnp.float32
BF16 = jnp.bfloat16
VMEM_LIMIT = 50 * 1024 * 1024


def dot_nn(a, b):
    return lax.dot_general(a, b, (((1,), (0,)), ((), ())), preferred_element_type=F32)


def dot_nt(a, b):
    return lax.dot_general(a, b, (((1,), (1,)), ((), ())), preferred_element_type=F32)


def dot_tn(a, b):
    return lax.dot_general(a, b, (((0,), (0,)), ((), ())), preferred_element_type=F32)


def flip(value, axis, size, bit):
    return lax.ppermute(value, axis, [(i, i ^ (1 << bit)) for i in range(size)])


def cube_gather(value, axis, size, bits):
    index = lax.axis_index(axis)
    done = []
    for bit in bits:
        other = flip(value, axis, size, bit)
        mine = (index >> bit) & 1
        low = jnp.where(mine == 0, value, other)
        high = jnp.where(mine == 0, other, value)
        place = sum(1 for b in done if b > bit)
        value = jnp.stack([low, high], axis=place)
        done.append(bit)
    return value.reshape((size,) + value.shape[len(done) :])


def cube_reduce(value, axis, size, bits):
    index = lax.axis_index(axis)
    left = list(range(len(bits)))[::-1]
    value = value.reshape((2,) * len(bits) + value.shape[1:])
    for bit in bits:
        place = left.index(bit)
        mine = (index >> bit) & 1
        sent = lax.dynamic_index_in_dim(value, 1 - mine, place, keepdims=False)
        kept = lax.dynamic_index_in_dim(value, mine, place, keepdims=False)
        got = flip(sent, axis, size, bit)
        value = (kept.astype(F32) + got.astype(F32)).astype(value.dtype)
        left.remove(bit)
    return value


def ring(value, size):
    return lax.ppermute(value, "seq", [(i, (i + 2) % size) for i in range(size)])


def swap(value, size):
    return lax.ppermute(value, "seq", [(i, i ^ 1) for i in range(size)])


class Gather:
    def __init__(self, value, size):
        self.size = size
        self.own, self.other = [value], [swap(value, size)]

    def launch(self):
        self.flight = ring(self.own[-1], self.size)

    def land(self, value):
        self.own.append(value)
        self.other.append(swap(value, self.size))

    def pieces(self):
        return self.own + self.other


class Scatter:
    def __init__(self, own, other, size):
        self.size, self.chips, self.mine = size, size // 2, own
        self.got = swap(other, size)
        self.step = 0

    def part(self):
        rows = self.mine.shape[0] // self.chips
        at = ((self.step + 1) % self.chips) * rows
        return self.mine[at : at + rows].astype(F32) + self.got[at : at + rows].astype(F32)

    def launch(self):
        total = self.part() if self.step == 0 else self.held.astype(F32) + self.part()
        self.flight = ring(total.astype(BF16), self.size)
        self.step += 1

    def land(self, value):
        self.held = value

    def total(self):
        return self.held.astype(F32) + self.part()


def launch(*hops):
    for hop in hops:
        hop.launch()


def land(*hops):
    for hop in hops:
        hop.land(hop.flight)


def tie(values, *hops):
    values, flights = lax.optimization_barrier((values, [hop.flight for hop in hops]))
    for hop, flight in zip(hops, flights):
        hop.land(flight)
    return values


def hold(values, other):
    return lax.optimization_barrier((values, other))


def turn(values, cosine, first, second):
    parts = []
    for at in range(0, values.shape[1], 128):
        part = values[:, at : at + 128]
        parts.append(
            part * cosine
            + pltpu.roll(part, 120, 1) * first
            + pltpu.roll(part, 8, 1) * second
        )
    return parts[0] if len(parts) == 1 else jnp.concatenate(parts, 1)


def head_stack(rows, heads):
    if heads == 1:
        return rows
    lane = lax.broadcasted_iota(jnp.int32, rows.shape, 1) // HEAD_DIM
    return jnp.concatenate(
        [jnp.where(lane == head, rows, jnp.zeros_like(rows)) for head in range(heads)], 0
    )


def head_rows(rows, heads, columns):
    if heads == 1:
        return rows
    return jnp.concatenate([rows[h : h + 1, columns] for h in range(heads)], 1)


def table_rows(ref, perm_ref, first, count, unit):
    parts = [
        ref[pl.ds(pl.multiple_of(perm_ref[first + n] * unit, unit), unit), :] for n in range(count)
    ]
    return jnp.concatenate(parts, 0)


def forward_kernel(
    heads,
    unit,
    group,
    block,
    pieces,
    perm_ref,
    *refs,
):
    x_refs = refs[:pieces]
    (
        w_ref, bias_ref, cos_ref, first_ref, second_ref, w_back_ref, scaled_ref, act_ref,
        slope_ref, q_ref, k_ref, v_ref, att_ref, lse_ref, attb_ref, own_ref, other_ref,
        x_ref, att_rows,
    ) = refs[pieces:]
    length = x_ref.shape[0]
    g = heads * HEAD_DIM
    count = group // unit
    for n in range(pieces):
        x_ref[n * unit : (n + 1) * unit, :] = x_refs[n][...]

    def project(step, carry):
        at = pl.multiple_of(step * group, group)
        rows = pl.ds(at, group)
        x = x_ref[rows, :].astype(F32)
        mean = jnp.mean(x, axis=1, keepdims=True)
        centred = x - mean
        variance = jnp.mean(centred * centred, axis=1, keepdims=True)
        scaled = (centred * lax.rsqrt(variance + EPSILON)).astype(BF16)
        scaled_ref[rows, :] = scaled
        made = dot_nn(scaled, w_ref[...]) + bias_ref[...]
        first = step * count
        cosine = table_rows(cos_ref, perm_ref, first, count, unit)
        one = table_rows(first_ref, perm_ref, first, count, unit)
        two = table_rows(second_ref, perm_ref, first, count, unit)
        turned = turn(made[:, : 2 * g], cosine, one, two)
        query = (turned[:, :g] * (HEAD_DIM**-0.5)).astype(BF16)
        keys = turned[:, g:].astype(BF16)
        values = made[:, 2 * g : 3 * g].astype(BF16)
        for n in range(count):
            to = pl.ds(pl.multiple_of(perm_ref[first + n] * unit, unit), unit)
            q_ref[to, :] = query[n * unit : (n + 1) * unit]
            k_ref[to, :] = keys[n * unit : (n + 1) * unit]
            v_ref[to, :] = values[n * unit : (n + 1) * unit]
        up = made[:, 3 * g :]
        phi = 0.5 * (1.0 + lax.erf(up * 0.7071067811865476))
        act_ref[rows, :] = (up * phi).astype(BF16)
        slope_ref[rows, :] = (
            phi + up * 0.3989422804014327 * jnp.exp(-0.5 * up * up)
        ).astype(BF16)
        return carry

    lax.fori_loop(0, length // group, project, 0)

    turned_v = v_ref[...].astype(F32).T.astype(BF16)
    key_at = lax.broadcasted_iota(jnp.int32, (block, heads * block), 0)
    query_at = lax.broadcasted_iota(jnp.int32, (block, heads * block), 1) % block
    allowed = key_at <= query_at
    for i in range(length // block):
        here = slice(i * block, (i + 1) * block)
        stack = head_stack(q_ref[here, :], heads)
        scores = [dot_nt(k_ref[n * block : (n + 1) * block, :], stack) for n in range(i + 1)]
        scores[i] = jnp.where(allowed, scores[i], NEGATIVE)
        peak = jnp.max(scores[0], axis=0, keepdims=True)
        for n in range(1, i + 1):
            peak = jnp.maximum(peak, jnp.max(scores[n], axis=0, keepdims=True))
        total = jnp.zeros_like(peak)
        mixed = jnp.zeros((g, heads * block), F32)
        for n in range(i + 1):
            weights = jnp.exp(scores[n] - peak)
            total = total + jnp.sum(weights, axis=0, keepdims=True)
            mixed = mixed + dot_nn(
                turned_v[:, n * block : (n + 1) * block], weights.astype(BF16)
            )
        mixed = mixed / total
        log_total = peak + jnp.log(total)
        parts = []
        for h in range(heads):
            span = slice(h * block, (h + 1) * block)
            parts.append(mixed[h * HEAD_DIM : (h + 1) * HEAD_DIM, span])
            lse_ref[h : h + 1, here] = log_total[:, span]
        attended = parts[0] if heads == 1 else jnp.concatenate(parts, 0)
        att_ref[:, here] = attended
        att_rows[here, :] = attended.T

    def finish(step, carry, into):
        rows = pl.ds(pl.multiple_of(step * group, group), group)
        attended = table_rows(att_rows, perm_ref, step * count, count, unit).astype(BF16)
        attb_ref[rows, :] = attended
        to = pl.ds(pl.multiple_of(lax.rem(step, half) * group, group), group)
        into[to, :] = (
            dot_nn(attended, w_back_ref[:g, :]) + dot_nn(act_ref[rows, :], w_back_ref[g:, :])
        ).astype(BF16)
        return carry

    half = length // group // 2
    lax.fori_loop(half, 2 * half, functools.partial(finish, into=other_ref), 0)
    lax.fori_loop(0, half, functools.partial(finish, into=own_ref), 0)


def backward_kernel(
    heads,
    unit,
    group,
    block,
    perm_ref,
    ga_rows,
    wt_ref,
    cos_ref,
    first_ref,
    second_ref,
    q_ref,
    k_ref,
    v_ref,
    att_ref,
    lse_ref,
    gup_ref,
    gp_ref,
    sums_ref,
    own_ref,
    other_ref,
    dq_rows,
    dk_rows,
    dv_rows,
):
    length = gup_ref.shape[0]
    g = heads * HEAD_DIM
    count = group // unit

    turned_k = k_ref[...].astype(F32).T.astype(BF16)
    key_at = lax.broadcasted_iota(jnp.int32, (block, heads * block), 0)
    query_at = lax.broadcasted_iota(jnp.int32, (block, heads * block), 1) % block
    allowed = key_at <= query_at
    for i in range(length // block):
        here = slice(i * block, (i + 1) * block)
        queries = head_stack(q_ref[here, :], heads)
        grad = ga_rows[here, :]
        grads = head_stack(grad.astype(BF16), heads)
        product = grad.T * att_ref[:, here]
        delta = [
            jnp.sum(product[h * HEAD_DIM : (h + 1) * HEAD_DIM], axis=0, keepdims=True)
            for h in range(heads)
        ]
        delta = delta[0] if heads == 1 else jnp.concatenate(delta, 1)
        log_total = [lse_ref[h : h + 1, here] for h in range(heads)]
        log_total = log_total[0] if heads == 1 else jnp.concatenate(log_total, 1)
        turned_q = [jnp.zeros((HEAD_DIM, block), F32) for _ in range(heads)]
        for n in range(i + 1):
            there = slice(n * block, (n + 1) * block)
            probs = jnp.exp(dot_nt(k_ref[there, :], queries) - log_total)
            if n == i:
                probs = jnp.where(allowed, probs, 0.0)
            grad_scores = (probs * (dot_nt(v_ref[there, :], grads) - delta)).astype(BF16)
            value_part = dot_nn(probs.astype(BF16), grads)
            key_part = dot_nn(grad_scores, queries)
            if n == i:
                dv_rows[there, :] = value_part
                dk_rows[there, :] = key_part
            else:
                dv_rows[there, :] += value_part
                dk_rows[there, :] += key_part
            for h in range(heads):
                turned_q[h] = turned_q[h] + dot_nn(
                    turned_k[h * HEAD_DIM : (h + 1) * HEAD_DIM, there],
                    grad_scores[:, h * block : (h + 1) * block],
                )
        whole = turned_q[0] if heads == 1 else jnp.concatenate(turned_q, 0)
        dq_rows[here, :] = whole.T * (HEAD_DIM**-0.5)

    sums_ref[...] = jnp.zeros_like(sums_ref)

    def finish(step, carry, into):
        rows = pl.ds(pl.multiple_of(step * group, group), group)
        first = step * count
        cosine = table_rows(cos_ref, perm_ref, first, count, unit)
        one = table_rows(first_ref, perm_ref, first, count, unit)
        two = table_rows(second_ref, perm_ref, first, count, unit)
        both = jnp.concatenate(
            [
                table_rows(dq_rows, perm_ref, first, count, unit),
                table_rows(dk_rows, perm_ref, first, count, unit),
            ],
            1,
        )
        both = turn(both, cosine, -one, -two)
        values = table_rows(dv_rows, perm_ref, first, count, unit)
        made = jnp.concatenate([both, values], 1)
        sums_ref[0:1, :] += jnp.sum(made, axis=0, keepdims=True)
        made = made.astype(BF16)
        gp_ref[rows, :] = made
        to = pl.ds(pl.multiple_of(lax.rem(step, half) * group, group), group)
        into[to, :] = (
            dot_nn(made, wt_ref[: 3 * g, :]) + dot_nn(gup_ref[rows, :], wt_ref[3 * g :, :])
        ).astype(BF16)
        return carry

    half = length // group // 2
    lax.fori_loop(half, 2 * half, functools.partial(finish, into=other_ref), 0)
    lax.fori_loop(0, half, functools.partial(finish, into=own_ref), 0)


def hidden_kernel(
    unit,
    group,
    pieces,
    first,
    last,
    perm_ref,
    *refs,
):
    g_refs = refs[:pieces]
    back_ref, slope_ref, act_ref, attb_ref, scaled_ref = refs[pieces : pieces + 5]
    at = pieces + 5
    if not first:
        old_back, old_up, old_sums = refs[at : at + 3]
        at += 3
    gup_ref, ga_ref, new_back, new_up, new_sums, g_ref = refs[at:]
    length = g_ref.shape[0]
    count = group // unit
    g = ga_ref.shape[1]
    for n in range(pieces):
        g_ref[n * unit : (n + 1) * unit, :] = g_refs[n][...]
    new_sums[...] = jnp.zeros_like(new_sums) if first else old_sums[...]

    def pull(step, carry):
        rows = pl.ds(pl.multiple_of(step * group, group), group)
        made = dot_nn(g_ref[rows, :], back_ref[...])
        for n in range(count):
            to = pl.ds(pl.multiple_of(perm_ref[step * count + n] * unit, unit), unit)
            ga_ref[to, :] = made[n * unit : (n + 1) * unit, :g]
        grad_up = made[:, g:] * slope_ref[rows, :].astype(F32)
        new_sums[0:1, :] += jnp.sum(grad_up, axis=0, keepdims=True)
        gup_ref[rows, :] = grad_up.astype(BF16)
        return carry

    lax.fori_loop(0, length // group, pull, 0)

    width = g_ref.shape[1]
    tile = 256
    for column in range(0, width, tile):
        there = slice(column, column + tile)
        up = dot_tn(scaled_ref[:, there], gup_ref[...])
        new_up[there, :] = up if first else up + old_up[there, :]
    both = jnp.concatenate([attb_ref[...], act_ref[...]], 1)
    if last:
        owners, cut = new_back.shape[0], new_back.shape[2]
    for row in range(0, both.shape[1], 128):
        here = slice(row, min(row + 128, both.shape[1]))
        part = dot_tn(both[:, here], g_ref[...])
        if not first:
            part = part + old_back[here, :]
        if last:
            for n in range(owners):
                new_back[n, here, :] = part[:, n * cut : (n + 1) * cut].astype(BF16)
        else:
            new_back[here, :] = part


def fold_kernel(cols, w_ref, norms_ref, extra_ref, back_ref, w_out, wt_out, bias_out, backt_out):
    turned = norms_ref[...].astype(F32).T
    w_out[:, :cols] = (w_ref[:, :cols].astype(F32) * turned[:, 0:1]).astype(BF16)
    w_out[:, cols:] = (w_ref[:, cols:].astype(F32) * turned[:, 2:3]).astype(BF16)
    wt_out[...] = w_out[...].T
    backt_out[...] = back_ref[...].T
    made = dot_nn(norms_ref[...], w_ref[...])
    bias_out[:, :cols] = made[1:2, :cols] + extra_ref[:, :cols].astype(F32)
    bias_out[:, cols:] = made[3:4, cols:] + extra_ref[:, cols:].astype(F32)


def kernel_call(body, outs, scratch, flops, args, scalars=1):
    specs = [pl.BlockSpec(memory_space=pltpu.SMEM)] * scalars + [
        pl.BlockSpec(memory_space=pltpu.VMEM) for _ in args[scalars:]
    ]
    size = sum(math.prod(a.shape) * a.dtype.itemsize for a in list(args) + list(outs))
    return pl.pallas_call(
        body,
        out_shape=tuple(outs),
        in_specs=specs,
        out_specs=tuple(pl.BlockSpec(memory_space=pltpu.VMEM) for _ in outs),
        scratch_shapes=scratch,
        compiler_params=pltpu.CompilerParams(vmem_limit_bytes=VMEM_LIMIT),
        cost_estimate=pl.CostEstimate(
            flops=int(flops), bytes_accessed=int(size), transcendentals=0
        ),
    )(*args)


def shaped(*shape, dtype=BF16):
    return jax.ShapeDtypeStruct(shape, dtype)


def rotary_tables(length):
    half = ROTARY // 2
    freqs = 10000.0 ** (-np.arange(half, dtype=np.float64) * 2.0 / ROTARY)
    angles = np.arange(length)[:, None] * freqs[None, :]
    cosine, sine = np.cos(angles), np.sin(angles)
    none = np.zeros_like(sine)
    rest = np.zeros((length, HEAD_DIM - ROTARY))
    cos_head = np.concatenate([cosine, cosine, rest + 1.0], 1)
    first = np.concatenate([-sine, none, rest], 1)
    second = np.concatenate([none, sine, rest], 1)
    return tuple(
        jnp.asarray(np.concatenate([t, t], 1).astype(np.float32)) for t in (cos_head, first, second)
    )


def split_heads(values, heads, back=False):
    lead = values.shape[:-1]
    shape = (3, heads, HEAD_DIM) if back else (heads, 3, HEAD_DIM)
    return jnp.swapaxes(values.reshape(lead + shape), -3, -2).reshape(values.shape)


def local(
    dp,
    seq,
    inputs,
    w_qkv,
    b_qkv,
    w_out,
    b_out,
    w_up,
    b_up,
    w_down,
    b_down,
    norm1_gain,
    norm1_shift,
    norm2_gain,
    norm2_shift,
    cotangent,
):
    span, count, width = inputs.shape
    length = span * seq
    chips = seq // 2
    qkv_cols = w_qkv.shape[1]
    heads = qkv_cols // (3 * HEAD_DIM)
    g = heads * HEAD_DIM
    dp_bits = list(range(dp.bit_length() - 1))
    seq_bits = list(range(seq.bit_length() - 1))
    me = lax.axis_index("seq")
    chip, core = me // 2, me % 2
    steps = jnp.arange(chips, dtype=jnp.int32)
    there = lax.rem(chip - steps + chips, chips) * 2
    perm = jnp.concatenate([there + core, there + 1 - core]).astype(jnp.int32)
    tables = rotary_tables(length)

    sources = [inputs[:, s] for s in range(count)]
    grads = [cotangent[:, s] for s in range(count)]

    norms = jnp.stack([norm1_gain, norm1_shift, norm2_gain, norm2_shift, b_out, b_down])
    small = jnp.concatenate([norms.reshape(-1), b_qkv, b_up])
    small = cube_gather(small, "dp", dp, dp_bits)
    in_block = jnp.concatenate([split_heads(w_qkv, heads), w_up], 1)
    out_block = jnp.concatenate([w_out, w_down], 0)
    w_in = cube_gather(in_block, "dp", dp, dp_bits).reshape(width, in_block.shape[1])
    w_back = cube_gather(out_block, "dp", dp, dp_bits[::-1])
    w_back = jnp.swapaxes(w_back, 0, 1).reshape(out_block.shape[0], width)
    norms = cube_gather(small[:, : norms.size], "seq", seq, seq_bits)
    norms = norms.reshape(seq, dp, 6, -1).transpose(2, 1, 0, 3).reshape(6, width)
    gain_one, shift_one, gain_two, shift_two, out_bias, down_bias = [
        norms[i].astype(F32) for i in range(6)
    ]
    at = 6 * norm1_gain.size
    qkv_bias = split_heads(small[:, at : at + b_qkv.size].reshape(-1), heads)
    up_bias = small[:, at + b_qkv.size :].reshape(-1)
    in_cols = w_in.shape[1]
    hidden = in_cols - qkv_cols
    folded, folded_t, bias, back_t = kernel_call(
        functools.partial(fold_kernel, qkv_cols),
        [
            shaped(width, in_cols),
            shaped(in_cols, width),
            shaped(1, in_cols, dtype=F32),
            shaped(width, g + hidden),
        ],
        [],
        1e7,
        (
            w_in,
            jnp.concatenate([norms, jnp.zeros((2, width), BF16)], 0),
            jnp.concatenate([qkv_bias, up_bias])[None],
            w_back,
        ),
        scalars=0,
    )

    unit = span
    group = math.gcd(length, 256)
    block = math.gcd(length, 256)
    matmul = 2.0 * length * width
    pairs = 2.0 * heads * length * length * 64

    def run_forward(pieces):
        return kernel_call(
            functools.partial(forward_kernel, heads, unit, group, block, len(pieces)),
            [
                shaped(length, width),
                shaped(length, hidden),
                shaped(length, hidden),
                shaped(length, g),
                shaped(length, g),
                shaped(length, g),
                shaped(g, length, dtype=F32),
                shaped(heads, length, dtype=F32),
                shaped(length, g),
                shaped(length // 2, width),
                shaped(length // 2, width),
            ],
            [pltpu.VMEM((length, width), BF16), pltpu.VMEM((length, g), F32)],
            matmul * (4 * g + 2 * hidden) + 8 * pairs,
            (perm, *pieces, folded, bias, *tables, w_back),
        )

    def run_hidden(pieces, f, old, last):
        back = shaped(dp, g + hidden, width // dp) if last else shaped(g + hidden, width, dtype=F32)
        return kernel_call(
            functools.partial(hidden_kernel, unit, group, len(pieces), not old, last),
            [
                shaped(length, hidden),
                shaped(length, g, dtype=F32),
                back,
                shaped(width, hidden, dtype=F32),
                shaped(8, hidden, dtype=F32),
            ],
            [pltpu.VMEM((length, width), BF16)],
            matmul * (2 * g + 3 * hidden),
            (perm, *pieces, back_t, f[2], f[1], f[8], f[0], *old),
        )

    def run_backward(f, made):
        return kernel_call(
            functools.partial(backward_kernel, heads, unit, group, block),
            [
                shaped(length, 3 * g),
                shaped(8, 3 * g, dtype=F32),
                shaped(length // 2, width),
                shaped(length // 2, width),
            ],
            [pltpu.VMEM((length, g), F32) for _ in range(3)],
            matmul * (3 * g + hidden) + 16 * pairs,
            (perm, made[1], folded_t, *tables, *f[3:8], made[0]),
        )

    hops = chips - 1
    x0, x1 = [Gather(source, seq) for source in sources]
    launch(x0, x1)
    for _ in range(hops - 1):
        land(x0)
        launch(x0)
        land(x1)
        launch(x1)
    land(x0)
    held, x0.own[-1] = hold(grads, x0.own[-1])
    g0, g1 = [Gather(grad, seq) for grad in held]
    launch(g0, g1)
    f0 = run_forward(x0.pieces())
    land(x1)
    pieces = tie(x1.pieces(), g0, g1)
    launch(g0, g1)
    o0 = Scatter(f0[9], f0[10], seq)
    f1 = run_forward(pieces)
    f1 = tie(f1, g0, g1)
    for _ in range(hops - 3):
        launch(g0, g1)
        land(g0, g1)
    launch(g0, g1, o0)
    o1 = Scatter(f1[9], f1[10], seq)
    land(g0)
    h0 = run_hidden(g0.pieces(), f0, (), False)
    h0, o1.got = hold(h0, o1.got)
    launch(o1)
    b0 = run_backward(f0, h0)
    land(g1)
    pieces, b0 = tie((g1.pieces(), b0), o0, o1)
    launch(o0, o1)
    p0 = Scatter(b0[2], b0[3], seq)
    h1 = run_hidden(pieces, f1, (h0[2], h0[3], h0[4]), True)
    h1 = tie(h1, o0)
    launch(o0, p0)
    b1 = run_backward(f1, h1)
    p1 = Scatter(b1[2], b1[3], seq)
    b1 = tie(b1, o1, o0, p0)
    launch(o1, p0)
    for _ in range(hops - 3):
        launch(o0)
        land(o0, o1)
        launch(o1)
    land(o1, p0)
    launch(p1, p0)
    for _ in range(hops - 3):
        land(p0, p1)
        launch(p0, p1)
    land(p1)
    launch(p1)
    land(p0, p1)
    launch(p1)
    land(p1)
    branches = [out.total() for out in (o0, o1)]
    pulled = [pull.total() for pull in (p0, p1)]
    forward, back = (f0, f1), (b0, b1)

    scaled_up, up_sums = h1[3], h1[4][0]
    scaled_qkv = sum(dot_tn(f[0], b[0]) for f, b in zip(forward, back))
    qkv_sums = sum(b[1][0] for b in back)
    wide = w_in.astype(F32)
    grad_back = cube_reduce(h1[2], "dp", dp, dp_bits)
    def to_owner(part, gain, shift, sums):
        made = gain[:, None] * part + shift[:, None] * sums[None]
        made = made.astype(BF16).reshape(dp, width // dp, -1)
        return cube_reduce(made, "dp", dp, dp_bits[::-1]).astype(F32)

    grad_w_up = to_owner(scaled_up, gain_two, shift_two, up_sums)
    grad_w_qkv = to_owner(scaled_qkv, gain_one, shift_one, qkv_sums)
    grad_w_qkv = split_heads(grad_w_qkv, heads, back=True)
    grad_w_out, grad_w_down = grad_back[:g].astype(F32), grad_back[g:].astype(F32)

    w_one, w_two = wide[:, :qkv_cols], wide[:, qkv_cols:]
    bias_sum = sum(jnp.sum(g_s.astype(F32), 0) for g_s in grads)
    vectors = jnp.stack(
        [
            jnp.sum(w_one * scaled_qkv, 1),
            jnp.sum(w_one * qkv_sums[None], 1),
            jnp.sum(w_two * scaled_up, 1),
            jnp.sum(w_two * up_sums[None], 1),
            bias_sum,
        ]
    )
    vectors = vectors.reshape(5, dp, seq, -1).transpose(1, 2, 0, 3).reshape(dp, -1)
    biases = jnp.concatenate(
        [
            split_heads(qkv_sums, heads, back=True).reshape(dp, -1),
            up_sums.reshape(dp, -1),
        ],
        1,
    )
    summed = cube_reduce(jnp.concatenate([vectors, biases], 1), "dp", dp, dp_bits)
    cut = vectors.shape[1]
    grad_b_qkv = summed[cut : cut + b_qkv.size]
    grad_b_up = summed[cut + b_qkv.size :]
    norms_out = cube_reduce(summed[:cut].reshape(seq, 5, -1), "seq", seq, seq_bits)

    outputs, grads_in = [], []
    for s in range(count):
        source = sources[s].astype(F32)
        outputs.append((source + branches[s] + (out_bias + down_bias)[None]).astype(BF16))
        mean = jnp.mean(source, 1, keepdims=True)
        centred = source - mean
        inverse = lax.rsqrt(jnp.mean(centred * centred, 1, keepdims=True) + EPSILON)
        scaled = centred * inverse
        e = pulled[s]
        middle = jnp.mean(e, 1, keepdims=True)
        along = jnp.mean(e * scaled, 1, keepdims=True)
        grads_in.append(
            (grads[s].astype(F32) + inverse * (e - middle - scaled * along)).astype(BF16)
        )
    return (
        jnp.stack(outputs, 1),
        jnp.stack(grads_in, 1),
        grad_w_qkv,
        grad_b_qkv,
        grad_w_out,
        norms_out[4],
        grad_w_up,
        grad_b_up,
        grad_w_down,
        norms_out[4],
        norms_out[0],
        norms_out[1],
        norms_out[2],
        norms_out[3],
    )


def solution(mesh):
    tokens = P("seq", "dp", None)
    rows, columns = P("dp", "seq"), P("seq", "dp")
    wide, flat = P(("seq", "dp")), P(("dp", "seq"))
    return jax.shard_map(
        functools.partial(local, mesh.shape["dp"], mesh.shape["seq"]),
        mesh=mesh,
        in_specs=(
            tokens, rows, wide, columns, flat, rows, wide, columns, flat, flat, flat, flat, flat,
            tokens,
        ),
        out_specs=(
            tokens, tokens, rows, wide, columns, flat, rows, wide, columns, flat, flat, flat,
            flat, flat,
        ),
        check_vma=False,
    )
```

```python
import functools
import math

import jax
import jax.numpy as jnp
import numpy as np
from jax import lax
from jax.experimental import pallas as pl
from jax.experimental.pallas import tpu as pltpu
from jax.sharding import PartitionSpec as P

HEAD_DIM = 64
ROTARY = 16
EPSILON = 1e-05
NEGATIVE = -1e30
F32 = jnp.float32
BF16 = jnp.bfloat16
VMEM_LIMIT = 50 * 1024 * 1024
COST = 1000


def dot_nn(a, b):
    return lax.dot_general(a, b, (((1,), (0,)), ((), ())), preferred_element_type=F32)


def dot_nt(a, b):
    return lax.dot_general(a, b, (((1,), (1,)), ((), ())), preferred_element_type=F32)


def dot_tn(a, b):
    return lax.dot_general(a, b, (((0,), (0,)), ((), ())), preferred_element_type=F32)


def cube(value, axis, bits):
    parts, masks, size = [value[None]], [0], 1 << len(bits)
    for bit in bits:
        sent = parts[0] if len(parts) == 1 else jnp.concatenate(parts, 0)
        parts.append(lax.ppermute(sent, axis, [(i, i ^ (1 << bit)) for i in range(size)]))
        masks = masks + [m ^ (1 << bit) for m in masks]
    return parts, masks


def cube_sum(value, axis, bits, markers=()):
    index, size = lax.axis_index(axis), 1 << len(bits)
    left = list(range(len(bits)))[::-1]
    rest = value.shape[1:]
    value = value.reshape((2,) * len(bits) + rest)
    for bit in bits:
        place = left.index(bit)
        mine = (index >> bit) & 1
        sent = lax.dynamic_index_in_dim(value, 1 - mine, place, keepdims=False)
        kept = lax.dynamic_index_in_dim(value, mine, place, keepdims=False)
        got = lax.ppermute(sent, axis, [(i, i ^ (1 << bit)) for i in range(size)])
        total = kept.astype(F32) + got.astype(F32)
        value = total.astype(value.dtype)
        if markers:
            value = after(value, *markers)
        left.remove(bit)
    return total


def cube_step(value, axis, size, bit):
    got = lax.ppermute(value, axis, [(i, i ^ (1 << bit)) for i in range(size)])
    mine = (lax.axis_index(axis) >> bit) & 1
    low, high = jnp.where(mine == 0, value, got), jnp.where(mine == 0, got, value)
    return jnp.concatenate([low, high], 0)


def after(values, *markers):
    return lax.optimization_barrier((values, markers))[0]


def turn(values, cosine, first, second):
    parts = []
    for at in range(0, values.shape[1], 128):
        part = values[:, at : at + 128]
        parts.append(
            part * cosine
            + pltpu.roll(part, 120, 1) * first
            + pltpu.roll(part, 8, 1) * second
        )
    return parts[0] if len(parts) == 1 else jnp.concatenate(parts, 1)


def head_stack(rows, heads):
    if heads == 1:
        return rows
    lane = lax.broadcasted_iota(jnp.int32, rows.shape, 1) // HEAD_DIM
    return jnp.concatenate(
        [jnp.where(lane == head, rows, jnp.zeros_like(rows)) for head in range(heads)], 0
    )


def head_rows(rows, heads, columns):
    if heads == 1:
        return rows
    return jnp.concatenate([rows[h : h + 1, columns] for h in range(heads)], 1)


def forward_kernel(
    heads, group, block, held, x_ref, w_ref, bias_ref, cos_ref, first_ref, second_ref,
    w_back_ref, *refs
):
    (
        scaled_ref, act_ref, slope_ref, q_ref, k_ref, v_ref, att_ref, lse_ref, attb_ref, out_ref,
    ) = refs[held:]
    unit = x_ref.shape[2]
    length = unit * x_ref.shape[0]
    g = heads * HEAD_DIM
    count = group // unit

    def project(step, carry):
        at = pl.multiple_of(step * group, group)
        rows = pl.ds(at, group)
        x = jnp.concatenate([x_ref[step * count + n, 0] for n in range(count)], 0).astype(F32)
        mean = jnp.mean(x, axis=1, keepdims=True)
        centred = x - mean
        variance = jnp.mean(centred * centred, axis=1, keepdims=True)
        scaled = (centred * lax.rsqrt(variance + EPSILON)).astype(BF16)
        scaled_ref[rows, :] = scaled
        made = dot_nn(scaled, w_ref[...]) + bias_ref[...]
        turned = turn(made[:, : 2 * g], cos_ref[rows, :], first_ref[rows, :], second_ref[rows, :])
        q_ref[rows, :] = (turned[:, :g] * (HEAD_DIM**-0.5)).astype(BF16)
        k_ref[rows, :] = turned[:, g:].astype(BF16)
        v_ref[rows, :] = made[:, 2 * g : 3 * g].astype(BF16)
        up = made[:, 3 * g :]
        phi = 0.5 * (1.0 + lax.erf(up * 0.7071067811865476))
        act_ref[rows, :] = (up * phi).astype(BF16)
        slope_ref[rows, :] = (
            phi + up * 0.3989422804014327 * jnp.exp(-0.5 * up * up)
        ).astype(BF16)
        return carry

    lax.fori_loop(0, length // group, project, 0)

    turned_v = v_ref[...].astype(F32).T.astype(BF16)
    key_at = lax.broadcasted_iota(jnp.int32, (block, heads * block), 0)
    query_at = lax.broadcasted_iota(jnp.int32, (block, heads * block), 1) % block
    allowed = key_at <= query_at
    for i in range(length // block):
        here = slice(i * block, (i + 1) * block)
        stack = head_stack(q_ref[here, :], heads)
        scores = [dot_nt(k_ref[n * block : (n + 1) * block, :], stack) for n in range(i + 1)]
        scores[i] = jnp.where(allowed, scores[i], NEGATIVE)
        peak = jnp.max(scores[0], axis=0, keepdims=True)
        for n in range(1, i + 1):
            peak = jnp.maximum(peak, jnp.max(scores[n], axis=0, keepdims=True))
        total = jnp.zeros_like(peak)
        mixed = jnp.zeros((g, heads * block), F32)
        for n in range(i + 1):
            weights = jnp.exp(scores[n] - peak)
            total = total + jnp.sum(weights, axis=0, keepdims=True)
            mixed = mixed + dot_nn(
                turned_v[:, n * block : (n + 1) * block], weights.astype(BF16)
            )
        mixed = mixed / total
        log_total = peak + jnp.log(total)
        parts = []
        for h in range(heads):
            span = slice(h * block, (h + 1) * block)
            parts.append(mixed[h * HEAD_DIM : (h + 1) * HEAD_DIM, span])
            lse_ref[h : h + 1, here] = log_total[:, span]
        attended = parts[0] if heads == 1 else jnp.concatenate(parts, 0)
        att_ref[:, here] = attended
        attb_ref[here, :] = attended.T.astype(BF16)

    count = group // unit

    def finish(step, carry):
        rows = pl.ds(pl.multiple_of(step * group, group), group)
        made = dot_nn(attb_ref[rows, :], w_back_ref[:g, :])
        made = made + dot_nn(act_ref[rows, :], w_back_ref[g:, :])
        made = made.astype(BF16)
        for n in range(count):
            out_ref[step * count + n, 0] = made[n * unit : (n + 1) * unit]
        return carry

    lax.fori_loop(0, length // group, finish, 0)


def backward_kernel(
    heads,
    unit,
    group,
    block,
    held,
    ga_rows,
    wt_ref,
    cos_ref,
    first_ref,
    second_ref,
    q_ref,
    k_ref,
    v_ref,
    att_ref,
    lse_ref,
    gup_ref,
    *refs,
):
    gp_ref, sums_ref, e_ref, dq_rows, dk_rows, dv_rows = refs[held:]
    length = gup_ref.shape[0]
    g = heads * HEAD_DIM
    count = group // unit

    turned_k = k_ref[...].astype(F32).T.astype(BF16)
    key_at = lax.broadcasted_iota(jnp.int32, (block, heads * block), 0)
    query_at = lax.broadcasted_iota(jnp.int32, (block, heads * block), 1) % block
    allowed = key_at <= query_at
    for i in range(length // block):
        here = slice(i * block, (i + 1) * block)
        queries = head_stack(q_ref[here, :], heads)
        grad = ga_rows[here, :]
        grads = head_stack(grad.astype(BF16), heads)
        product = grad.T * att_ref[:, here]
        delta = [
            jnp.sum(product[h * HEAD_DIM : (h + 1) * HEAD_DIM], axis=0, keepdims=True)
            for h in range(heads)
        ]
        delta = delta[0] if heads == 1 else jnp.concatenate(delta, 1)
        log_total = [lse_ref[h : h + 1, here] for h in range(heads)]
        log_total = log_total[0] if heads == 1 else jnp.concatenate(log_total, 1)
        turned_q = [jnp.zeros((HEAD_DIM, block), F32) for _ in range(heads)]
        for n in range(i + 1):
            there = slice(n * block, (n + 1) * block)
            probs = jnp.exp(dot_nt(k_ref[there, :], queries) - log_total)
            if n == i:
                probs = jnp.where(allowed, probs, 0.0)
            grad_scores = (probs * (dot_nt(v_ref[there, :], grads) - delta)).astype(BF16)
            value_part = dot_nn(probs.astype(BF16), grads)
            key_part = dot_nn(grad_scores, queries)
            if n == i:
                dv_rows[there, :] = value_part
                dk_rows[there, :] = key_part
            else:
                dv_rows[there, :] += value_part
                dk_rows[there, :] += key_part
            for h in range(heads):
                turned_q[h] = turned_q[h] + dot_nn(
                    turned_k[h * HEAD_DIM : (h + 1) * HEAD_DIM, there],
                    grad_scores[:, h * block : (h + 1) * block],
                )
        whole = turned_q[0] if heads == 1 else jnp.concatenate(turned_q, 0)
        dq_rows[here, :] = whole.T * (HEAD_DIM**-0.5)

    sums_ref[...] = jnp.zeros_like(sums_ref)

    def finish(step, carry):
        rows = pl.ds(pl.multiple_of(step * group, group), group)
        both = jnp.concatenate([dq_rows[rows, :], dk_rows[rows, :]], 1)
        both = turn(both, cos_ref[rows, :], -first_ref[rows, :], -second_ref[rows, :])
        made = jnp.concatenate([both, dv_rows[rows, :]], 1)
        sums_ref[0:1, :] += jnp.sum(made, axis=0, keepdims=True)
        made = made.astype(BF16)
        gp_ref[rows, :] = made
        pulled = dot_nn(made, wt_ref[: 3 * g, :]) + dot_nn(gup_ref[rows, :], wt_ref[3 * g :, :])
        pulled = pulled.astype(BF16)
        for n in range(count):
            e_ref[step * count + n, 0] = pulled[n * unit : (n + 1) * unit]
        return carry

    lax.fori_loop(0, length // group, finish, 0)


def hidden_kernel(group, first, last, gathered_ref, *refs):
    back_ref, slope_ref, act_ref, attb_ref, scaled_ref = refs[:5]
    at = 5
    if not first:
        old_back, old_up, old_sums = refs[at : at + 3]
        at += 3
    if last:
        raw_ref, norms_ref = refs[at : at + 2]
        at += 2
    if last:
        gup_ref, ga_ref, new_back, new_sums, *rest, g_ref = refs[at:]
    else:
        gup_ref, ga_ref, new_back, new_up, new_sums, g_ref = refs[at:]
    length, width = g_ref.shape
    g = ga_ref.shape[1]
    unit = gathered_ref.shape[2]
    for n in range(gathered_ref.shape[0]):
        g_ref[n * unit : (n + 1) * unit, :] = gathered_ref[n, 0]
    new_sums[...] = jnp.zeros_like(new_sums) if first else old_sums[...]

    def pull(step, carry):
        rows = pl.ds(pl.multiple_of(step * group, group), group)
        made = dot_nn(g_ref[rows, :], back_ref[...])
        ga_ref[rows, :] = made[:, :g]
        grad_up = made[:, g:] * slope_ref[rows, :].astype(F32)
        new_sums[0:1, :] += jnp.sum(grad_up, axis=0, keepdims=True)
        gup_ref[rows, :] = grad_up.astype(BF16)
        return carry

    lax.fori_loop(0, length // group, pull, 0)

    tile = 256
    both_rows = attb_ref.shape[1] + act_ref.shape[1]
    if last:
        start = raw_ref.shape[1] - gup_ref.shape[1]
        turned = norms_ref[...].astype(F32).T
    for column in range(0, width, tile):
        there = slice(column, column + tile)
        up = dot_tn(scaled_ref[:, there], gup_ref[...])
        if not first:
            up = up + old_up[there, :]
        if last:
            raw = raw_ref[there, start:].astype(F32)
            made = owner_part(
                up, raw, new_sums[0:1, :], turned[there, 2:3], turned[there, 3:4], there, rest[0]
            )
            owner_rows(made, column, new_back, both_rows)
        else:
            new_up[there, :] = up
    both = jnp.concatenate([attb_ref[...], act_ref[...]], 1)
    if last:
        owners, cut = new_back.shape[0], new_back.shape[2]
    for row in range(0, both.shape[1], 128):
        here = slice(row, min(row + 128, both.shape[1]))
        part = dot_tn(both[:, here], g_ref[...])
        if not first:
            part = part + old_back[here, :]
        if last:
            for n in range(owners):
                new_back[n, here, :] = part[:, n * cut : (n + 1) * cut].astype(BF16)
        else:
            new_back[here, :] = part


def owner_rows(made, row, grad_ref, base):
    cut = grad_ref.shape[2]
    folds = made.shape[1] // cut
    rows = (grad_ref.shape[1] - base) // folds
    for at in range(0, made.shape[0], min(rows, made.shape[0])):
        count = min(rows, made.shape[0])
        owner, inner = (row + at) // rows, (row + at) % rows
        for fold in range(folds):
            to = base + fold * rows + inner
            grad_ref[owner, to : to + count, :] = made[
                at : at + count, fold * cut : (fold + 1) * cut
            ]


def owner_part(part, raw, sums, gain, shift, there, vectors_ref):
    made = (gain * part + shift * sums).astype(BF16)
    along = jnp.sum(raw * part, axis=1, keepdims=True)
    flat = jnp.sum(raw * sums, axis=1, keepdims=True)
    lane = lax.broadcasted_iota(jnp.int32, (part.shape[0], 128), 1)
    both = jnp.where(lane == 0, along, jnp.where(lane == 1, flat, 0.0))
    vectors_ref[:, there] = both.T[0:8, :]
    return made


def project_kernel(
    sequences, raw_ref, norms_ref, *refs
):
    scaled_refs, gp_refs, sum_refs = [refs[n * sequences : (n + 1) * sequences] for n in range(3)]
    grad_ref, vectors_ref, sums_ref = refs[3 * sequences :]
    width, cols = grad_ref.shape
    sums_ref[...] = sum(ref[...] for ref in sum_refs)
    turned = norms_ref[...].astype(F32).T
    tile = 256
    for column in range(0, width, tile):
        there = slice(column, column + tile)
        part = sum(dot_tn(s[:, there], gp[...]) for s, gp in zip(scaled_refs, gp_refs))
        grad_ref[there, :] = owner_part(
            part, raw_ref[there, :cols].astype(F32), sums_ref[0:1, :], turned[there, 0:1],
            turned[there, 1:2], there, vectors_ref,
        )


def fold_kernel(cols, pieces, place_ref, *refs):
    in_refs, back_refs = refs[:pieces], refs[pieces : 2 * pieces]
    norms_ref, extra_ref, raw_ref, w_out, wt_out, bias_out, back_out, backt_out = refs[2 * pieces :]
    rows, part = in_refs[0].shape[1], back_refs[0].shape[2]
    at = 0
    for in_ref, back_ref in zip(in_refs, back_refs):
        for n in range(in_ref.shape[0]):
            to = pl.multiple_of(place_ref[0, at] * rows, rows)
            raw_ref[pl.ds(to, rows), :] = in_ref[n]
            to = pl.multiple_of(place_ref[1, at] * part, part)
            backt_out[pl.ds(to, part), :] = back_ref[n].T
            at += 1
    turned = norms_ref[...].astype(F32).T
    w_out[:, :cols] = (raw_ref[:, :cols].astype(F32) * turned[:, 0:1]).astype(BF16)
    w_out[:, cols:] = (raw_ref[:, cols:].astype(F32) * turned[:, 2:3]).astype(BF16)
    wt_out[...] = w_out[...].T
    back_out[...] = backt_out[...].T
    made = dot_nn(norms_ref[...], raw_ref[...])
    bias_out[:, :cols] = made[1:2, :cols] + extra_ref[:, :cols].astype(F32)
    bias_out[:, cols:] = made[3:4, cols:] + extra_ref[:, cols:].astype(F32)


def kernel_call(body, outs, scratch, flops, args, scalars=1, own_specs=None, alias=None):
    specs = [pl.BlockSpec(memory_space=pltpu.SMEM)] * scalars + [
        pl.BlockSpec(memory_space=pltpu.VMEM) for _ in (*args[scalars:], *outs)
    ]
    for at, spec in (own_specs or {}).items():
        specs[at] = spec
    size = sum(math.prod(a.shape) * a.dtype.itemsize for a in list(args) + list(outs))
    return pl.pallas_call(
        body,
        grid=(1,) if own_specs else (),
        out_shape=tuple(outs),
        in_specs=specs[: len(args)],
        out_specs=tuple(specs[len(args) :]),
        scratch_shapes=scratch,
        input_output_aliases=alias or {},
        compiler_params=pltpu.CompilerParams(vmem_limit_bytes=VMEM_LIMIT),
        cost_estimate=pl.CostEstimate(
            flops=int(flops) // COST, bytes_accessed=int(size) // COST, transcendentals=0
        ),
    )(*args)


def shaped(*shape, dtype=BF16):
    return jax.ShapeDtypeStruct(shape, dtype)


def rotary_tables(length):
    half = ROTARY // 2
    freqs = 10000.0 ** (-np.arange(half, dtype=np.float64) * 2.0 / ROTARY)
    angles = np.arange(length)[:, None] * freqs[None, :]
    cosine, sine = np.cos(angles), np.sin(angles)
    none = np.zeros_like(sine)
    rest = np.zeros((length, HEAD_DIM - ROTARY))
    cos_head = np.concatenate([cosine, cosine, rest + 1.0], 1)
    first = np.concatenate([-sine, none, rest], 1)
    second = np.concatenate([none, sine, rest], 1)
    return tuple(
        jnp.asarray(np.concatenate([t, t], 1).astype(np.float32)) for t in (cos_head, first, second)
    )


def split_heads(values, heads, back=False):
    lead = values.shape[:-1]
    shape = (3, heads, HEAD_DIM) if back else (heads, 3, HEAD_DIM)
    return jnp.swapaxes(values.reshape(lead + shape), -3, -2).reshape(values.shape)


def local(
    dp,
    seq,
    inputs,
    w_qkv,
    b_qkv,
    w_out,
    b_out,
    w_up,
    b_up,
    w_down,
    b_down,
    norm1_gain,
    norm1_shift,
    norm2_gain,
    norm2_shift,
    cotangent,
):
    span, count, width = inputs.shape
    length = span * seq
    qkv_cols = w_qkv.shape[1]
    heads = qkv_cols // (3 * HEAD_DIM)
    g = heads * HEAD_DIM
    me = lax.axis_index("seq")
    tables = rotary_tables(length)

    sources = jnp.swapaxes(inputs, 0, 1)
    norms = jnp.stack([norm1_gain, norm1_shift, norm2_gain, norm2_shift, b_out, b_down])
    small = jnp.concatenate([norms.reshape(-1), b_qkv, b_up])
    dp_bits = list(range(dp.bit_length() - 1))
    seq_bits = list(range(seq.bit_length() - 1))
    (blocks, small), sources = lax.optimization_barrier(
        (((w_qkv, w_up, w_out, w_down), small), sources)
    )
    gathered_x = lax.all_gather(sources, "seq", axis=0)
    small = small[None]
    for bit in dp_bits:
        small = cube_step(small, "dp", dp, bit)
    size = norms.size
    norms = small[:, :size][None]
    norms = cube_step(norms, "seq", seq, seq_bits[0])
    in_block = jnp.concatenate([split_heads(blocks[0], heads), blocks[1]], 1)
    out_block = jnp.concatenate(blocks[2:], 0)
    in_pieces, in_masks = cube(in_block, "dp", dp_bits)
    out_pieces, out_masks = cube(out_block, "dp", dp_bits[::-1])
    place = jnp.asarray([in_masks, out_masks], jnp.int32) ^ lax.axis_index("dp")
    at = 6 * norm1_gain.size
    qkv_bias = split_heads(small[:, at : at + b_qkv.size].reshape(-1), heads)
    up_bias = small[:, at + b_qkv.size :].reshape(-1)
    in_cols, back_rows = in_block.shape[1], out_block.shape[0]
    hidden = in_cols - qkv_cols
    for bit in seq_bits[1:]:
        norms = cube_step(norms, "seq", seq, bit)
    norms = norms.reshape(seq, dp, 6, -1).transpose(2, 1, 0, 3).reshape(6, width)
    out_bias, down_bias = norms[4].astype(F32), norms[5].astype(F32)
    norms = jnp.concatenate([norms, jnp.zeros((2, width), BF16)], 0)
    grads = jnp.swapaxes(cotangent, 0, 1)
    gathered = lax.all_gather(after(grads, in_pieces[1]), "seq", axis=0)
    raw, folded, folded_t, bias, w_back, back_t = kernel_call(
        functools.partial(fold_kernel, qkv_cols, len(in_pieces)),
        [
            shaped(width, in_cols),
            shaped(width, in_cols),
            shaped(in_cols, width),
            shaped(1, in_cols, dtype=F32),
            shaped(back_rows, width),
            shaped(width, back_rows),
        ],
        [],
        1e7,
        (
            place,
            *in_pieces,
            *out_pieces,
            norms,
            jnp.concatenate([qkv_bias, up_bias])[None],
        ),
    )

    unit = span
    group = math.gcd(length, 256)
    block = math.gcd(length, 256)
    matmul = 2.0 * length * width
    pairs = 2.0 * heads * length * length * 64

    def of_sequence(s):
        return pl.BlockSpec((seq, 1, unit, width), lambda i: (0, s, 0, 0))

    def call_held(body, outs, scratch, flops, args, s, place, held, more=()):
        args = (*args, *held)
        own = {at: of_sequence(s) for at in (len(args) + place, *more)}
        if held:
            own[len(args) - 1] = pl.BlockSpec(memory_space=pl.ANY)
        return kernel_call(
            body, outs, scratch, flops, args, scalars=0, own_specs=own,
            alias={len(args) - 1: place} if held else None,
        )

    def run_forward(s, *held):
        return call_held(
            functools.partial(forward_kernel, heads, group, block, len(held)),
            [
                shaped(length, width),
                shaped(length, hidden),
                shaped(length, hidden),
                shaped(length, g),
                shaped(length, g),
                shaped(length, g),
                shaped(g, length, dtype=F32),
                shaped(heads, length, dtype=F32),
                shaped(length, g),
                shaped(seq, count, unit, width),
            ],
            [],
            matmul * (4 * g + 2 * hidden) + 8 * pairs,
            (gathered_x, folded, bias, *tables, w_back),
            s,
            9,
            held,
            (0,),
        )

    def run_hidden(s, f, old, last):
        cut = width // dp
        if last:
            wide = [
                shaped(dp, back_rows + hidden, cut),
                shaped(8, hidden, dtype=F32),
                shaped(8, width, dtype=F32),
            ]
        else:
            wide = [
                shaped(back_rows, width, dtype=F32),
                shaped(width, hidden, dtype=F32),
                shaped(8, hidden, dtype=F32),
            ]
        return kernel_call(
            functools.partial(hidden_kernel, group, not old, last),
            [shaped(length, hidden), shaped(length, g, dtype=F32)] + wide,
            [pltpu.VMEM((length, width), BF16)],
            matmul * (2 * g + 3 * hidden),
            (gathered, back_t, f[2], f[1], f[8], f[0], *old) + ((raw, norms) if last else ()),
            scalars=0,
            own_specs={0: of_sequence(s)},
        )

    def run_backward(s, f, made, *held):
        return call_held(
            functools.partial(backward_kernel, heads, unit, group, block, len(held)),
            [
                shaped(length, 3 * g),
                shaped(8, 3 * g, dtype=F32),
                shaped(seq, count, unit, width),
            ],
            [pltpu.VMEM((length, g), F32) for _ in range(3)],
            matmul * (3 * g + hidden) + 16 * pairs,
            (made[1], folded_t, *tables, *f[3:8], made[0]),
            s,
            2,
            held,
        )

    f0 = run_forward(0)
    f1 = run_forward(1, f0[9])
    branches = lax.psum_scatter(f1[9], "seq", scatter_dimension=0)
    sources, grads = after((sources, grads), f1[7])
    late_sums = sum(jnp.sum(grad.astype(F32), 0) for grad in grads)
    h0 = run_hidden(0, f0, (), False)
    b0 = run_backward(0, f0, h0)
    h1 = run_hidden(1, f1, (h0[2], h0[3], h0[4]), True)
    b1 = run_backward(1, f1, h1, b0[2])
    pulled = lax.psum_scatter(b1[2], "seq", scatter_dimension=0)
    token, branches = lax.optimization_barrier((norms, branches))
    grad_qkv, norm_one, qkv_sums = kernel_call(
        functools.partial(project_kernel, count),
        [
            shaped(width, qkv_cols),
            shaped(8, width, dtype=F32),
            shaped(8, qkv_cols, dtype=F32),
        ],
        [],
        matmul * 3 * g * count,
        (raw, token, f0[0], f1[0], b0[0], b1[0], b0[1], b1[1]),
        scalars=0,
    )
    qkv_sums = qkv_sums[0]
    rows = width // dp
    vectors = jnp.concatenate([norm_one[:2], h1[4][:2], late_sums[None]], 0)
    vectors = vectors.reshape(5, dp, seq, -1).transpose(1, 2, 0, 3).reshape(dp, -1)
    cut = vectors.shape[1]
    biases = [split_heads(qkv_sums, heads, back=True).reshape(dp, -1), h1[3][0].reshape(dp, -1)]
    vectors = jnp.concatenate([vectors] + biases, 1)
    summed = cube_sum(vectors, "dp", dp_bits)
    grad_b_qkv, grad_b_up = summed[cut : cut + b_qkv.size], summed[cut + b_qkv.size :]
    norms_out = cube_sum(summed[:cut].reshape(seq, 5, -1), "seq", seq_bits)

    done = cube_sum(h1[2], "dp", dp_bits, (qkv_sums,))
    grad_w_out, grad_w_down = done[:g], done[g:back_rows]
    grad_w_up = jnp.concatenate(
        [done[at : at + rows] for at in range(back_rows, done.shape[0], rows)], 1
    )
    grad_w_qkv = cube_sum(grad_qkv.reshape(dp, rows, -1), "dp", dp_bits[::-1])
    grad_w_qkv = split_heads(grad_w_qkv, heads, back=True)

    outputs, grads_in = [], []
    for s in range(count):
        source = sources[s].astype(F32)
        outputs.append((source + branches[s].astype(F32) + (out_bias + down_bias)[None]).astype(BF16))
        mean = jnp.mean(source, 1, keepdims=True)
        centred = source - mean
        inverse = lax.rsqrt(jnp.mean(centred * centred, 1, keepdims=True) + EPSILON)
        scaled = centred * inverse
        e = pulled[s].astype(F32)
        middle = jnp.mean(e, 1, keepdims=True)
        along = jnp.mean(e * scaled, 1, keepdims=True)
        grads_in.append(
            (grads[s].astype(F32) + inverse * (e - middle - scaled * along)).astype(BF16)
        )
    return (
        jnp.stack(outputs, 1),
        jnp.stack(grads_in, 1),
        grad_w_qkv,
        grad_b_qkv,
        grad_w_out,
        norms_out[4],
        grad_w_up,
        grad_b_up,
        grad_w_down,
        norms_out[4],
        norms_out[0],
        norms_out[1],
        norms_out[2],
        norms_out[3],
    )


def solution(mesh):
    tokens = P("seq", "dp", None)
    rows, columns = P("dp", "seq"), P("seq", "dp")
    wide, flat = P(("seq", "dp")), P(("dp", "seq"))
    return jax.shard_map(
        functools.partial(local, mesh.shape["dp"], mesh.shape["seq"]),
        mesh=mesh,
        in_specs=(
            tokens, rows, wide, columns, flat, rows, wide, columns, flat, flat, flat, flat, flat,
            tokens,
        ),
        out_specs=(
            tokens, tokens, rows, wide, columns, flat, rows, wide, columns, flat, flat, flat,
            flat, flat,
        ),
        check_vma=False,
    )
```

```python
import functools
import math

import jax
import jax.numpy as jnp
import numpy as np
from jax import lax
from jax.experimental import pallas as pl
from jax.experimental.pallas import tpu as pltpu
from jax.sharding import PartitionSpec as P

HEAD_DIM = 64
ROTARY = 16
EPSILON = 1e-05
NEGATIVE = -1e30
F32 = jnp.float32
BF16 = jnp.bfloat16
VMEM_LIMIT = 63 * 1024 * 1024
COST = 1000


def dot_nn(a, b):
    return lax.dot_general(a, b, (((1,), (0,)), ((), ())), preferred_element_type=F32)


def dot_nt(a, b):
    return lax.dot_general(a, b, (((1,), (1,)), ((), ())), preferred_element_type=F32)


def dot_tn(a, b):
    return lax.dot_general(a, b, (((0,), (0,)), ((), ())), preferred_element_type=F32)


def cube(parts, axis, size, bit):
    sent = parts[0] if len(parts) == 1 else jnp.concatenate(parts, 0)
    return parts + [lax.ppermute(sent, axis, [(i, i ^ (1 << bit)) for i in range(size)])]


def cube_masks(bits):
    masks = [0]
    for bit in bits:
        masks = masks + [m ^ (1 << bit) for m in masks]
    return masks


def cube_sum(value, axis, bits):
    return CubeSum(value, axis, bits).finish()


def cube_step(value, axis, size, bit):
    got = lax.ppermute(value, axis, [(i, i ^ (1 << bit)) for i in range(size)])
    mine = (lax.axis_index(axis) >> bit) & 1
    low, high = jnp.where(mine == 0, value, got), jnp.where(mine == 0, got, value)
    return jnp.concatenate([low, high], 0)


def tie(*values):
    return lax.optimization_barrier(values)


class CubeSum:
    def __init__(self, value, axis, bits):
        self.axis, self.bits, self.dtype = axis, list(bits), value.dtype
        self.left = sorted(bits, reverse=True)
        self.size = 1 << len(self.bits)
        self.value = value.reshape((2,) * len(self.bits) + value.shape[1:])

    def ready(self):
        bit = self.bits[0]
        place = self.left.index(bit)
        mine = (lax.axis_index(self.axis) >> bit) & 1
        self.kept = lax.dynamic_index_in_dim(self.value, mine, place, keepdims=False)
        return lax.dynamic_index_in_dim(self.value, 1 - mine, place, keepdims=False)

    def send(self, sent):
        bit = self.bits.pop(0)
        self.left.remove(bit)
        self.got = lax.ppermute(sent, self.axis, [(i, i ^ (1 << bit)) for i in range(self.size)])

    def land(self):
        self.total = self.kept.astype(F32) + self.got.astype(F32)
        self.value = self.total.astype(self.dtype)

    def finish(self):
        while self.bits:
            self.send(self.ready())
            self.land()
        return self.total


def turn(values, cosine, first, second):
    parts = []
    for at in range(0, values.shape[1], 128):
        part = values[:, at : at + 128]
        parts.append(
            part * cosine
            + pltpu.roll(part, 120, 1) * first
            + pltpu.roll(part, 8, 1) * second
        )
    return parts[0] if len(parts) == 1 else jnp.concatenate(parts, 1)


def head_stack(rows, heads):
    if heads == 1:
        return rows
    lane = lax.broadcasted_iota(jnp.int32, rows.shape, 1) // HEAD_DIM
    return jnp.concatenate(
        [jnp.where(lane == head, rows, jnp.zeros_like(rows)) for head in range(heads)], 0
    )


def head_rows(rows, heads, columns):
    if heads == 1:
        return rows
    return jnp.concatenate([rows[h : h + 1, columns] for h in range(heads)], 1)


def forward_kernel(
    heads, group, block, held, token_ref, x_ref, w_ref, bias_ref, cos_ref, first_ref, second_ref,
    w_back_ref, *refs
):
    (
        scaled_ref, act_ref, slope_ref, q_ref, k_ref, v_ref, att_ref, lse_ref, attb_ref, out_ref,
    ) = refs[held:]
    unit = x_ref.shape[2]
    length = unit * x_ref.shape[0]
    g = heads * HEAD_DIM
    count = group // unit

    def project(step, carry):
        at = pl.multiple_of(step * group, group)
        rows = pl.ds(at, group)
        x = jnp.concatenate([x_ref[step * count + n, 0] for n in range(count)], 0).astype(F32)
        mean = jnp.mean(x, axis=1, keepdims=True)
        centred = x - mean
        variance = jnp.mean(centred * centred, axis=1, keepdims=True)
        scaled = (centred * lax.rsqrt(variance + EPSILON)).astype(BF16)
        scaled_ref[rows, :] = scaled
        made = dot_nn(scaled, w_ref[...]) + bias_ref[...]
        turned = turn(made[:, : 2 * g], cos_ref[rows, :], first_ref[rows, :], second_ref[rows, :])
        q_ref[rows, :] = (turned[:, :g] * (HEAD_DIM**-0.5)).astype(BF16)
        k_ref[rows, :] = turned[:, g:].astype(BF16)
        v_ref[rows, :] = made[:, 2 * g : 3 * g].astype(BF16)
        up = made[:, 3 * g :]
        phi = 0.5 * (1.0 + lax.erf(up * 0.7071067811865476))
        act_ref[rows, :] = (up * phi).astype(BF16)
        slope_ref[rows, :] = (
            phi + up * 0.3989422804014327 * jnp.exp(-0.5 * up * up)
        ).astype(BF16)
        return carry

    lax.fori_loop(0, length // group, project, 0)

    turned_v = v_ref[...].astype(F32).T.astype(BF16)
    key_at = lax.broadcasted_iota(jnp.int32, (block, heads * block), 0)
    query_at = lax.broadcasted_iota(jnp.int32, (block, heads * block), 1) % block
    allowed = key_at <= query_at
    for i in range(length // block):
        here = slice(i * block, (i + 1) * block)
        stack = head_stack(q_ref[here, :], heads)
        scores = [dot_nt(k_ref[n * block : (n + 1) * block, :], stack) for n in range(i + 1)]
        scores[i] = jnp.where(allowed, scores[i], NEGATIVE)
        peak = jnp.max(scores[0], axis=0, keepdims=True)
        for n in range(1, i + 1):
            peak = jnp.maximum(peak, jnp.max(scores[n], axis=0, keepdims=True))
        total = jnp.zeros_like(peak)
        mixed = jnp.zeros((g, heads * block), F32)
        for n in range(i + 1):
            weights = jnp.exp(scores[n] - peak)
            total = total + jnp.sum(weights, axis=0, keepdims=True)
            mixed = mixed + dot_nn(
                turned_v[:, n * block : (n + 1) * block], weights.astype(BF16)
            )
        mixed = mixed / total
        log_total = peak + jnp.log(total)
        parts = []
        for h in range(heads):
            span = slice(h * block, (h + 1) * block)
            parts.append(mixed[h * HEAD_DIM : (h + 1) * HEAD_DIM, span])
            lse_ref[h : h + 1, here] = log_total[:, span]
        attended = parts[0] if heads == 1 else jnp.concatenate(parts, 0)
        att_ref[:, here] = attended
        attb_ref[here, :] = attended.T.astype(BF16)

    def finish(step, carry):
        rows = pl.ds(pl.multiple_of(step * group, group), group)
        made = dot_nn(attb_ref[rows, :], w_back_ref[:g, :])
        made = (made + dot_nn(act_ref[rows, :], w_back_ref[g:, :])).astype(BF16)
        for n in range(count):
            out_ref[step * count + n, 0] = made[n * unit : (n + 1) * unit]
        return carry

    lax.fori_loop(0, length // group, finish, 0)


def backward_kernel(
    heads,
    group,
    unit,
    block,
    held,
    token_ref,
    ga_rows,
    wt_ref,
    cos_ref,
    first_ref,
    second_ref,
    q_ref,
    k_ref,
    v_ref,
    att_ref,
    lse_ref,
    gup_ref,
    *refs,
):
    gp_ref, sums_ref, e_ref, dq_rows, dk_rows, dv_rows = refs[held:]
    count = group // unit
    length = gup_ref.shape[0]
    g = heads * HEAD_DIM

    turned_k = k_ref[...].astype(F32).T.astype(BF16)
    key_at = lax.broadcasted_iota(jnp.int32, (block, heads * block), 0)
    query_at = lax.broadcasted_iota(jnp.int32, (block, heads * block), 1) % block
    allowed = key_at <= query_at
    for i in range(length // block):
        here = slice(i * block, (i + 1) * block)
        queries = head_stack(q_ref[here, :], heads)
        grad = ga_rows[here, :]
        grads = head_stack(grad.astype(BF16), heads)
        product = grad.T * att_ref[:, here]
        delta = [
            jnp.sum(product[h * HEAD_DIM : (h + 1) * HEAD_DIM], axis=0, keepdims=True)
            for h in range(heads)
        ]
        delta = delta[0] if heads == 1 else jnp.concatenate(delta, 1)
        log_total = [lse_ref[h : h + 1, here] for h in range(heads)]
        log_total = log_total[0] if heads == 1 else jnp.concatenate(log_total, 1)
        turned_q = [jnp.zeros((HEAD_DIM, block), F32) for _ in range(heads)]
        for n in range(i + 1):
            there = slice(n * block, (n + 1) * block)
            probs = jnp.exp(dot_nt(k_ref[there, :], queries) - log_total)
            if n == i:
                probs = jnp.where(allowed, probs, 0.0)
            grad_scores = (probs * (dot_nt(v_ref[there, :], grads) - delta)).astype(BF16)
            value_part = dot_nn(probs.astype(BF16), grads)
            key_part = dot_nn(grad_scores, queries)
            if n == i:
                dv_rows[there, :] = value_part
                dk_rows[there, :] = key_part
            else:
                dv_rows[there, :] += value_part
                dk_rows[there, :] += key_part
            for h in range(heads):
                turned_q[h] = turned_q[h] + dot_nn(
                    turned_k[h * HEAD_DIM : (h + 1) * HEAD_DIM, there],
                    grad_scores[:, h * block : (h + 1) * block],
                )
        whole = turned_q[0] if heads == 1 else jnp.concatenate(turned_q, 0)
        dq_rows[here, :] = whole.T * (HEAD_DIM**-0.5)

    sums_ref[...] = jnp.zeros_like(sums_ref)

    def finish(step, carry):
        rows = pl.ds(pl.multiple_of(step * group, group), group)
        both = jnp.concatenate([dq_rows[rows, :], dk_rows[rows, :]], 1)
        both = turn(both, cos_ref[rows, :], -first_ref[rows, :], -second_ref[rows, :])
        made = jnp.concatenate([both, dv_rows[rows, :]], 1)
        sums_ref[0:1, :] += jnp.sum(made, axis=0, keepdims=True)
        made = made.astype(BF16)
        gp_ref[rows, :] = made
        pulled = dot_nn(made, wt_ref[: 3 * g, :]) + dot_nn(gup_ref[rows, :], wt_ref[3 * g :, :])
        pulled = pulled.astype(BF16)
        for n in range(count):
            e_ref[step * count + n, 0] = pulled[n * unit : (n + 1) * unit]
        return carry

    lax.fori_loop(0, length // group, finish, 0)


def hidden_kernel(group, first, last, token_ref, gathered_ref, *refs):
    back_ref, slope_ref, act_ref, attb_ref, scaled_ref = refs[:5]
    at = 5
    if not first:
        old_back, old_up, old_sums = refs[at : at + 3]
        at += 3
    if last:
        raw_ref, norms_ref = refs[at : at + 2]
        at += 2
    if last:
        gup_ref, ga_ref, new_back, new_up, new_sums, vectors_ref, g_ref = refs[at:]
    else:
        gup_ref, ga_ref, new_back, new_up, new_sums, g_ref = refs[at:]
    length, width = g_ref.shape
    g = ga_ref.shape[1]
    unit = gathered_ref.shape[2]
    for n in range(gathered_ref.shape[0]):
        g_ref[n * unit : (n + 1) * unit, :] = gathered_ref[n, 0]
    new_sums[...] = jnp.zeros_like(new_sums) if first else old_sums[...]

    def pull(step, carry):
        rows = pl.ds(pl.multiple_of(step * group, group), group)
        made = dot_nn(g_ref[rows, :], back_ref[...])
        ga_ref[rows, :] = made[:, :g]
        grad_up = made[:, g:] * slope_ref[rows, :].astype(F32)
        new_sums[0:1, :] += jnp.sum(grad_up, axis=0, keepdims=True)
        gup_ref[rows, :] = grad_up.astype(BF16)
        return carry

    lax.fori_loop(0, length // group, pull, 0)

    tile = 256
    if last:
        start = raw_ref.shape[1] - gup_ref.shape[1]
        turned = norms_ref[...].astype(F32).T
    for column in range(0, width, tile):
        there = slice(column, column + tile)
        up = dot_tn(scaled_ref[:, there], gup_ref[...])
        if not first:
            up = up + old_up[there, :]
        if last:
            raw = raw_ref[there, start:].astype(F32)
            made = owner_part(
                up, raw, new_sums[0:1, :], turned[there, 2:3], turned[there, 3:4], there,
                vectors_ref,
            )
            owner_rows(made, column, new_up)
        else:
            new_up[there, :] = up
    both = jnp.concatenate([attb_ref[...], act_ref[...]], 1)
    if last:
        owners, cut = new_back.shape[0], new_back.shape[2]
    for row in range(0, both.shape[1], 128):
        here = slice(row, min(row + 128, both.shape[1]))
        part = dot_tn(both[:, here], g_ref[...])
        if not first:
            part = part + old_back[here, :]
        if last:
            for n in range(owners):
                new_back[n, here, :] = part[:, n * cut : (n + 1) * cut].astype(BF16)
        else:
            new_back[here, :] = part


def owner_rows(made, row, grad_ref):
    rows = grad_ref.shape[1]
    count = min(rows, made.shape[0])
    for at in range(0, made.shape[0], count):
        owner, inner = (row + at) // rows, (row + at) % rows
        grad_ref[owner, inner : inner + count, :] = made[at : at + count]


def owner_part(part, raw, sums, gain, shift, there, vectors_ref):
    made = (gain * part + shift * sums).astype(BF16)
    along = jnp.sum(raw * part, axis=1, keepdims=True)
    flat = jnp.sum(raw * sums, axis=1, keepdims=True)
    lane = lax.broadcasted_iota(jnp.int32, (part.shape[0], 128), 1)
    both = jnp.where(lane == 0, along, jnp.where(lane == 1, flat, 0.0))
    vectors_ref[:, there] = both.T[0:8, :]
    return made


def project_kernel(
    sequences, token_ref, raw_ref, norms_ref, *refs
):
    scaled_refs, gp_refs, sum_refs = [refs[n * sequences : (n + 1) * sequences] for n in range(3)]
    grad_ref, vectors_ref, sums_ref = refs[3 * sequences :]
    width, cols = raw_ref.shape[0], grad_ref.shape[2]
    sums_ref[...] = sum(ref[...] for ref in sum_refs)
    turned = norms_ref[...].astype(F32).T
    tile = 256
    for column in range(0, width, tile):
        there = slice(column, column + tile)
        part = sum(dot_tn(s[:, there], gp[...]) for s, gp in zip(scaled_refs, gp_refs))
        made = owner_part(
            part, raw_ref[there, :cols].astype(F32), sums_ref[0:1, :], turned[there, 0:1],
            turned[there, 1:2], there, vectors_ref,
        )
        owner_rows(made, column, grad_ref)


def fold_kernel(cols, pieces, place_ref, *refs):
    in_refs, back_refs = refs[:pieces], refs[pieces : 2 * pieces]
    norms_ref, extra_ref, raw_ref, w_out, wt_out, bias_out, back_out, backt_out = refs[2 * pieces :]
    rows, part = in_refs[0].shape[1], back_refs[0].shape[2]
    at = 0
    for in_ref, back_ref in zip(in_refs, back_refs):
        for n in range(in_ref.shape[0]):
            to = pl.multiple_of(place_ref[0, at] * rows, rows)
            raw_ref[pl.ds(to, rows), :] = in_ref[n]
            to = pl.multiple_of(place_ref[1, at] * part, part)
            backt_out[pl.ds(to, part), :] = back_ref[n].T
            at += 1
    turned = norms_ref[...].astype(F32).T
    w_out[:, :cols] = (raw_ref[:, :cols].astype(F32) * turned[:, 0:1]).astype(BF16)
    w_out[:, cols:] = (raw_ref[:, cols:].astype(F32) * turned[:, 2:3]).astype(BF16)
    wt_out[...] = w_out[...].T
    back_out[...] = backt_out[...].T
    made = dot_nn(norms_ref[...], raw_ref[...])
    bias_out[:, :cols] = made[1:2, :cols] + extra_ref[:, :cols].astype(F32)
    bias_out[:, cols:] = made[3:4, cols:] + extra_ref[:, cols:].astype(F32)


def kernel_call(body, outs, scratch, flops, args, scalars=1, own_specs=None, alias=None):
    specs = [pl.BlockSpec(memory_space=pltpu.SMEM)] * scalars + [
        pl.BlockSpec(memory_space=pltpu.VMEM) for _ in (*args[scalars:], *outs)
    ]
    for at, spec in (own_specs or {}).items():
        specs[at] = spec
    size = sum(math.prod(a.shape) * a.dtype.itemsize for a in list(args) + list(outs))
    return pl.pallas_call(
        body,
        grid=(1,) if own_specs else (),
        out_shape=tuple(outs),
        in_specs=specs[: len(args)],
        out_specs=tuple(specs[len(args) :]),
        scratch_shapes=scratch,
        input_output_aliases=alias or {},
        compiler_params=pltpu.CompilerParams(vmem_limit_bytes=VMEM_LIMIT),
        cost_estimate=pl.CostEstimate(
            flops=int(flops) // COST, bytes_accessed=int(size) // COST, transcendentals=0
        ),
    )(*args)


def shaped(*shape, dtype=BF16):
    return jax.ShapeDtypeStruct(shape, dtype)


def rotary_tables(length):
    half = ROTARY // 2
    freqs = 10000.0 ** (-np.arange(half, dtype=np.float64) * 2.0 / ROTARY)
    angles = np.arange(length)[:, None] * freqs[None, :]
    cosine, sine = np.cos(angles), np.sin(angles)
    none = np.zeros_like(sine)
    rest = np.zeros((length, HEAD_DIM - ROTARY))
    cos_head = np.concatenate([cosine, cosine, rest + 1.0], 1)
    first = np.concatenate([-sine, none, rest], 1)
    second = np.concatenate([none, sine, rest], 1)
    return tuple(
        jnp.asarray(np.concatenate([t, t], 1).astype(np.float32)) for t in (cos_head, first, second)
    )


def split_heads(values, heads, back=False):
    lead = values.shape[:-1]
    shape = (3, heads, HEAD_DIM) if back else (heads, 3, HEAD_DIM)
    return jnp.swapaxes(values.reshape(lead + shape), -3, -2).reshape(values.shape)


def local(
    dp,
    seq,
    inputs,
    w_qkv,
    b_qkv,
    w_out,
    b_out,
    w_up,
    b_up,
    w_down,
    b_down,
    norm1_gain,
    norm1_shift,
    norm2_gain,
    norm2_shift,
    cotangent,
):
    span, count, width = inputs.shape
    length = span * seq
    qkv_cols = w_qkv.shape[1]
    heads = qkv_cols // (3 * HEAD_DIM)
    g = heads * HEAD_DIM
    me = lax.axis_index("seq")
    token = jnp.zeros((8,), jnp.int32)
    tables = rotary_tables(length)

    sources = jnp.swapaxes(inputs, 0, 1)
    norms = jnp.stack([norm1_gain, norm1_shift, norm2_gain, norm2_shift, b_out, b_down])
    small = jnp.concatenate([norms.reshape(-1), b_qkv, b_up])
    dp_bits = list(range(dp.bit_length() - 1))
    seq_bits = list(range(seq.bit_length() - 1))
    (blocks, small), sources = lax.optimization_barrier(
        (((w_qkv, w_up, w_out, w_down), small), sources)
    )
    gathered_x = lax.all_gather(sources, "seq", axis=0)
    in_block = jnp.concatenate([split_heads(blocks[0], heads), blocks[1]], 1)
    out_block = jnp.concatenate(blocks[2:], 0)
    small = small[None]
    for bit in dp_bits:
        small = cube_step(small, "dp", dp, bit)
    small, late = tie(small, cotangent)
    grads = jnp.swapaxes(late, 0, 1)
    gathered = lax.all_gather(grads, "seq", axis=0)
    in_pieces, out_pieces = [in_block[None]], [out_block[None]]
    for bit, back in zip(dp_bits, dp_bits[::-1]):
        in_pieces = cube(in_pieces, "dp", dp, bit)
        out_pieces = cube(out_pieces, "dp", dp, back)
    in_masks, out_masks = cube_masks(dp_bits), cube_masks(dp_bits[::-1])
    size = norms.size
    norms = small[:, :size][None]
    norms = cube_step(norms, "seq", seq, seq_bits[0])
    place = jnp.asarray([in_masks, out_masks], jnp.int32) ^ lax.axis_index("dp")
    at = 6 * norm1_gain.size
    qkv_bias = split_heads(small[:, at : at + b_qkv.size].reshape(-1), heads)
    up_bias = small[:, at + b_qkv.size :].reshape(-1)
    in_cols, back_rows = in_block.shape[1], out_block.shape[0]
    hidden = in_cols - qkv_cols
    for bit in seq_bits[1:]:
        norms = cube_step(norms, "seq", seq, bit)
    norms = norms.reshape(seq, dp, 6, -1).transpose(2, 1, 0, 3).reshape(6, width)
    out_bias, down_bias = norms[4].astype(F32), norms[5].astype(F32)
    norms = jnp.concatenate([norms, jnp.zeros((2, width), BF16)], 0)
    raw, folded, folded_t, bias, w_back, back_t = kernel_call(
        functools.partial(fold_kernel, qkv_cols, len(in_pieces)),
        [
            shaped(width, in_cols),
            shaped(width, in_cols),
            shaped(in_cols, width),
            shaped(1, in_cols, dtype=F32),
            shaped(back_rows, width),
            shaped(width, back_rows),
        ],
        [],
        1e7,
        (
            place,
            *in_pieces,
            *out_pieces,
            norms,
            jnp.concatenate([qkv_bias, up_bias])[None],
        ),
    )

    unit = span
    group = math.gcd(length, 256)
    block = math.gcd(length, 256)
    matmul = 2.0 * length * width
    pairs = 2.0 * heads * length * length * 64

    def of_sequence(s):
        return pl.BlockSpec((seq, 1, unit, width), lambda i: (0, s, 0, 0))

    def call_held(body, outs, scratch, flops, args, s, place, held, more=()):
        args = (*args, *held)
        own = {at: of_sequence(s) for at in (len(args) + place, *more)}
        if held:
            own[len(args) - 1] = pl.BlockSpec(memory_space=pl.ANY)
        return kernel_call(
            body, outs, scratch, flops, args, own_specs=own,
            alias={len(args) - 1: place} if held else None,
        )

    def run_forward(token, s, *held):
        return call_held(
            functools.partial(forward_kernel, heads, group, block, len(held)),
            [
                shaped(length, width),
                shaped(length, hidden),
                shaped(length, hidden),
                shaped(length, g),
                shaped(length, g),
                shaped(length, g),
                shaped(g, length, dtype=F32),
                shaped(heads, length, dtype=F32),
                shaped(length, g),
                shaped(seq, count, unit, width),
            ],
            [],
            matmul * (4 * g + 2 * hidden) + 8 * pairs,
            (token, gathered_x, folded, bias, *tables, w_back),
            s,
            9,
            held,
            (1,),
        )

    def run_hidden(token, s, gathered, f, old, last):
        cut = width // dp
        if last:
            wide = [
                shaped(dp, back_rows, cut),
                shaped(dp, cut, hidden),
                shaped(8, hidden, dtype=F32),
                shaped(8, width, dtype=F32),
            ]
        else:
            wide = [
                shaped(back_rows, width, dtype=F32),
                shaped(width, hidden, dtype=F32),
                shaped(8, hidden, dtype=F32),
            ]
        return kernel_call(
            functools.partial(hidden_kernel, group, not old, last),
            [shaped(length, hidden), shaped(length, g, dtype=F32)] + wide,
            [pltpu.VMEM((length, width), BF16)],
            matmul * (2 * g + 3 * hidden),
            (token, gathered, back_t, f[2], f[1], f[8], f[0], *old)
            + ((raw, norms) if last else ()),
            own_specs={1: of_sequence(s)},
        )

    def run_backward(token, s, f, made, *held):
        return call_held(
            functools.partial(backward_kernel, heads, group, unit, block, len(held)),
            [
                shaped(length, 3 * g),
                shaped(8, 3 * g, dtype=F32),
                shaped(seq, count, unit, width),
            ],
            [pltpu.VMEM((length, g), F32) for _ in range(3)],
            matmul * (3 * g + hidden) + 16 * pairs,
            (token, made[1], folded_t, *tables, *f[3:8], made[0]),
            s,
            2,
            held,
        )

    f0 = run_forward(token, 0)
    f1 = run_forward(token, 1, f0[9])
    branches = lax.psum_scatter(f1[9], "seq", scatter_dimension=0)
    (sources, grads), f1_lse = tie((sources, grads), f1[7])
    f1 = (*f1[:7], f1_lse, *f1[8:])
    late_sums = sum(jnp.sum(grad.astype(F32), 0) for grad in grads)
    h0 = run_hidden(token, 0, gathered, f0, (), False)
    b0 = run_backward(token, 0, f0, h0)
    token, b0_sums = tie(token, b0[1])
    h1 = run_hidden(token, 1, gathered, f1, h0[2:5], True)
    early = [CubeSum(h1[2], "dp", dp_bits[::-1]), CubeSum(h1[3], "dp", dp_bits)]
    token, sent = tie(token, [blocks.ready() for blocks in early])
    for blocks, value in zip(early, sent):
        blocks.send(value)
    b1 = run_backward(token, 1, f1, h1, b0[2])
    token, b1, gots = tie(token, b1, [blocks.got for blocks in early])
    for blocks, got in zip(early, gots):
        blocks.got = got
        blocks.land()
    b1_sums = b1[1]
    e = lax.psum_scatter(b1[2], "seq", scatter_dimension=0)
    grad_qkv, norm_one, qkv_sums = kernel_call(
        functools.partial(project_kernel, count),
        [
            shaped(dp, width // dp, qkv_cols),
            shaped(8, width, dtype=F32),
            shaped(8, qkv_cols, dtype=F32),
        ],
        [],
        matmul * 3 * g * count,
        (token, raw, norms, f0[0], f1[0], b0[0], b1[0], b0_sums, b1_sums),
    )
    last_qkv = CubeSum(grad_qkv, "dp", dp_bits)
    last_qkv.send(last_qkv.ready())
    last_qkv.land()
    qkv_sums = qkv_sums[0]
    rows = width // dp
    vectors = jnp.concatenate([norm_one[:2], h1[5][:2], late_sums[None]], 0)
    vectors = vectors.reshape(5, dp, seq, -1).transpose(1, 2, 0, 3).reshape(dp, -1)
    cut = vectors.shape[1]
    biases = [split_heads(qkv_sums, heads, back=True).reshape(dp, -1), h1[4][0].reshape(dp, -1)]
    vectors = jnp.concatenate([vectors] + biases, 1)
    summed = cube_sum(vectors, "dp", dp_bits)
    grad_b_qkv, grad_b_up = summed[cut : cut + b_qkv.size], summed[cut + b_qkv.size :]
    summed, branches = tie(summed, branches)
    last = CubeSum(summed[:cut].reshape(seq, 5, -1), "seq", seq_bits)
    norms_out = last.finish()
    output = jnp.stack(
        [
            (sources[s].astype(F32) + branches[s].astype(F32) + (out_bias + down_bias)[None])
            .astype(BF16)
            for s in range(count)
        ],
        1,
    )
    output, norms_out, pulled = tie(output, norms_out, e)

    done = early[0].finish()
    grad_w_out, grad_w_down = done[:g], done[g:]
    grad_w_up = early[1].finish()
    grad_w_qkv = last_qkv.finish()
    grad_w_qkv = split_heads(grad_w_qkv, heads, back=True)

    grads_in = []
    for s in range(count):
        source = sources[s].astype(F32)
        mean = jnp.mean(source, 1, keepdims=True)
        centred = source - mean
        inverse = lax.rsqrt(jnp.mean(centred * centred, 1, keepdims=True) + EPSILON)
        scaled = centred * inverse
        e = pulled[s].astype(F32)
        middle = jnp.mean(e, 1, keepdims=True)
        along = jnp.mean(e * scaled, 1, keepdims=True)
        grads_in.append(
            (grads[s].astype(F32) + inverse * (e - middle - scaled * along)).astype(BF16)
        )
    return (
        output,
        jnp.stack(grads_in, 1),
        grad_w_qkv,
        grad_b_qkv,
        grad_w_out,
        norms_out[4],
        grad_w_up,
        grad_b_up,
        grad_w_down,
        norms_out[4],
        norms_out[0],
        norms_out[1],
        norms_out[2],
        norms_out[3],
    )


def solution(mesh):
    tokens = P("seq", "dp", None)
    rows, columns = P("dp", "seq"), P("seq", "dp")
    wide, flat = P(("seq", "dp")), P(("dp", "seq"))
    return jax.shard_map(
        functools.partial(local, mesh.shape["dp"], mesh.shape["seq"]),
        mesh=mesh,
        in_specs=(
            tokens, rows, wide, columns, flat, rows, wide, columns, flat, flat, flat, flat, flat,
            tokens,
        ),
        out_specs=(
            tokens, tokens, rows, wide, columns, flat, rows, wide, columns, flat, flat, flat,
            flat, flat,
        ),
        check_vma=False,
    )
```

```python
import functools
import math

import jax
import jax.numpy as jnp
import numpy as np
from jax import lax
from jax.experimental import pallas as pl
from jax.experimental.pallas import tpu as pltpu
from jax.sharding import PartitionSpec as P

HEAD_DIM = 64
ROTARY = 16
EPSILON = 1e-05
NEGATIVE = -1e30
F32 = jnp.float32
BF16 = jnp.bfloat16
VMEM_LIMIT = 56 * 1024 * 1024
COST = 1000


def dot_nn(a, b):
    return lax.dot_general(a, b, (((1,), (0,)), ((), ())), preferred_element_type=F32)


def dot_nt(a, b):
    return lax.dot_general(a, b, (((1,), (1,)), ((), ())), preferred_element_type=F32)


def dot_tn(a, b):
    return lax.dot_general(a, b, (((0,), (0,)), ((), ())), preferred_element_type=F32)


def cube(parts, axis, size, bit):
    sent = parts[0] if len(parts) == 1 else jnp.concatenate(parts, 0)
    return parts + [lax.ppermute(sent, axis, [(i, i ^ (1 << bit)) for i in range(size)])]


def cube_masks(bits):
    masks = [0]
    for bit in bits:
        masks = masks + [m ^ (1 << bit) for m in masks]
    return masks


def cube_sum(value, axis, bits):
    return CubeSum(value, axis, bits).finish()


def cube_step(value, axis, size, bit):
    got = lax.ppermute(value, axis, [(i, i ^ (1 << bit)) for i in range(size)])
    mine = (lax.axis_index(axis) >> bit) & 1
    low, high = jnp.where(mine == 0, value, got), jnp.where(mine == 0, got, value)
    return jnp.concatenate([low, high], 0)


def tie(*values):
    return lax.optimization_barrier(values)


class CubeSum:
    def __init__(self, value, axis, bits):
        self.axis, self.bits, self.dtype = axis, list(bits), value.dtype
        self.left = sorted(bits, reverse=True)
        self.size = 1 << len(self.bits)
        self.value = value.reshape((2,) * len(self.bits) + value.shape[1:])

    def ready(self):
        bit = self.bits[0]
        place = self.left.index(bit)
        mine = (lax.axis_index(self.axis) >> bit) & 1
        self.kept = lax.dynamic_index_in_dim(self.value, mine, place, keepdims=False)
        return lax.dynamic_index_in_dim(self.value, 1 - mine, place, keepdims=False)

    def send(self, sent):
        bit = self.bits.pop(0)
        self.left.remove(bit)
        self.got = lax.ppermute(sent, self.axis, [(i, i ^ (1 << bit)) for i in range(self.size)])

    def land(self):
        self.total = self.kept.astype(F32) + self.got.astype(F32)
        self.value = self.total.astype(self.dtype)

    def finish(self):
        while self.bits:
            self.send(self.ready())
            self.land()
        return self.total


def turn(values, cosine, first, second):
    parts = []
    for at in range(0, values.shape[1], 128):
        part = values[:, at : at + 128]
        parts.append(
            part * cosine
            + pltpu.roll(part, 120, 1) * first
            + pltpu.roll(part, 8, 1) * second
        )
    return parts[0] if len(parts) == 1 else jnp.concatenate(parts, 1)


def head_stack(rows, heads):
    if heads == 1:
        return rows
    lane = lax.broadcasted_iota(jnp.int32, rows.shape, 1) // HEAD_DIM
    return jnp.concatenate(
        [jnp.where(lane == head, rows, jnp.zeros_like(rows)) for head in range(heads)], 0
    )


def head_rows(rows, heads, columns):
    if heads == 1:
        return rows
    return jnp.concatenate([rows[h : h + 1, columns] for h in range(heads)], 1)


def forward_kernel(
    heads, group, block, held, token_ref, x_ref, w_ref, bias_ref, cos_ref, first_ref, second_ref,
    w_back_ref, *refs
):
    (
        scaled_ref, act_ref, slope_ref, q_ref, k_ref, v_ref, att_ref, lse_ref, attb_ref, out_ref,
    ) = refs[held:]
    unit = x_ref.shape[2]
    length = unit * x_ref.shape[0]
    g = heads * HEAD_DIM
    count = group // unit

    def project(step, carry):
        at = pl.multiple_of(step * group, group)
        rows = pl.ds(at, group)
        x = jnp.concatenate([x_ref[step * count + n, 0] for n in range(count)], 0).astype(F32)
        mean = jnp.mean(x, axis=1, keepdims=True)
        centred = x - mean
        variance = jnp.mean(centred * centred, axis=1, keepdims=True)
        scaled = (centred * lax.rsqrt(variance + EPSILON)).astype(BF16)
        scaled_ref[rows, :] = scaled
        made = dot_nn(scaled, w_ref[...]) + bias_ref[...]
        turned = turn(made[:, : 2 * g], cos_ref[rows, :], first_ref[rows, :], second_ref[rows, :])
        q_ref[rows, :] = (turned[:, :g] * (HEAD_DIM**-0.5)).astype(BF16)
        k_ref[rows, :] = turned[:, g:].astype(BF16)
        v_ref[rows, :] = made[:, 2 * g : 3 * g].astype(BF16)
        up = made[:, 3 * g :]
        phi = 0.5 * (1.0 + lax.erf(up * 0.7071067811865476))
        act_ref[rows, :] = (up * phi).astype(BF16)
        slope_ref[rows, :] = (
            phi + up * 0.3989422804014327 * jnp.exp(-0.5 * up * up)
        ).astype(BF16)
        return carry

    lax.fori_loop(0, length // group, project, 0)

    turned_v = v_ref[...].astype(F32).T.astype(BF16)
    key_at = lax.broadcasted_iota(jnp.int32, (block, heads * block), 0)
    query_at = lax.broadcasted_iota(jnp.int32, (block, heads * block), 1) % block
    allowed = key_at <= query_at
    for i in range(length // block):
        here = slice(i * block, (i + 1) * block)
        stack = head_stack(q_ref[here, :], heads)
        scores = [dot_nt(k_ref[n * block : (n + 1) * block, :], stack) for n in range(i + 1)]
        scores[i] = jnp.where(allowed, scores[i], NEGATIVE)
        peak = jnp.max(scores[0], axis=0, keepdims=True)
        for n in range(1, i + 1):
            peak = jnp.maximum(peak, jnp.max(scores[n], axis=0, keepdims=True))
        total = jnp.zeros_like(peak)
        mixed = jnp.zeros((g, heads * block), F32)
        for n in range(i + 1):
            weights = jnp.exp(scores[n] - peak)
            total = total + jnp.sum(weights, axis=0, keepdims=True)
            mixed = mixed + dot_nn(
                turned_v[:, n * block : (n + 1) * block], weights.astype(BF16)
            )
        mixed = mixed / total
        log_total = peak + jnp.log(total)
        parts = []
        for h in range(heads):
            span = slice(h * block, (h + 1) * block)
            parts.append(mixed[h * HEAD_DIM : (h + 1) * HEAD_DIM, span])
            lse_ref[h : h + 1, here] = log_total[:, span]
        attended = parts[0] if heads == 1 else jnp.concatenate(parts, 0)
        att_ref[:, here] = attended
        attb_ref[here, :] = attended.T.astype(BF16)

    def finish(step, carry):
        rows = pl.ds(pl.multiple_of(step * group, group), group)
        made = dot_nn(attb_ref[rows, :], w_back_ref[:g, :])
        made = (made + dot_nn(act_ref[rows, :], w_back_ref[g:, :])).astype(BF16)
        for n in range(count):
            out_ref[step * count + n, 0] = made[n * unit : (n + 1) * unit]
        return carry

    lax.fori_loop(0, length // group, finish, 0)


def backward_kernel(
    heads,
    group,
    unit,
    block,
    held,
    token_ref,
    ga_rows,
    wt_ref,
    cos_ref,
    first_ref,
    second_ref,
    q_ref,
    k_ref,
    v_ref,
    att_ref,
    lse_ref,
    gup_ref,
    *refs,
):
    gp_ref, sums_ref, e_ref, dq_rows, dk_rows, dv_rows = refs[held:]
    count = group // unit
    length = gup_ref.shape[0]
    g = heads * HEAD_DIM

    turned_k = k_ref[...].astype(F32).T.astype(BF16)
    key_at = lax.broadcasted_iota(jnp.int32, (block, heads * block), 0)
    query_at = lax.broadcasted_iota(jnp.int32, (block, heads * block), 1) % block
    allowed = key_at <= query_at
    for i in range(length // block):
        here = slice(i * block, (i + 1) * block)
        queries = head_stack(q_ref[here, :], heads)
        grad = ga_rows[here, :]
        grads = head_stack(grad.astype(BF16), heads)
        product = grad.T * att_ref[:, here]
        delta = [
            jnp.sum(product[h * HEAD_DIM : (h + 1) * HEAD_DIM], axis=0, keepdims=True)
            for h in range(heads)
        ]
        delta = delta[0] if heads == 1 else jnp.concatenate(delta, 1)
        log_total = [lse_ref[h : h + 1, here] for h in range(heads)]
        log_total = log_total[0] if heads == 1 else jnp.concatenate(log_total, 1)
        turned_q = [jnp.zeros((HEAD_DIM, block), F32) for _ in range(heads)]
        for n in range(i + 1):
            there = slice(n * block, (n + 1) * block)
            probs = jnp.exp(dot_nt(k_ref[there, :], queries) - log_total)
            if n == i:
                probs = jnp.where(allowed, probs, 0.0)
            grad_scores = (probs * (dot_nt(v_ref[there, :], grads) - delta)).astype(BF16)
            value_part = dot_nn(probs.astype(BF16), grads)
            key_part = dot_nn(grad_scores, queries)
            if n == i:
                dv_rows[there, :] = value_part
                dk_rows[there, :] = key_part
            else:
                dv_rows[there, :] += value_part
                dk_rows[there, :] += key_part
            for h in range(heads):
                turned_q[h] = turned_q[h] + dot_nn(
                    turned_k[h * HEAD_DIM : (h + 1) * HEAD_DIM, there],
                    grad_scores[:, h * block : (h + 1) * block],
                )
        whole = turned_q[0] if heads == 1 else jnp.concatenate(turned_q, 0)
        dq_rows[here, :] = whole.T * (HEAD_DIM**-0.5)

    sums_ref[...] = jnp.zeros_like(sums_ref)

    def finish(step, carry):
        rows = pl.ds(pl.multiple_of(step * group, group), group)
        both = jnp.concatenate([dq_rows[rows, :], dk_rows[rows, :]], 1)
        both = turn(both, cos_ref[rows, :], -first_ref[rows, :], -second_ref[rows, :])
        made = jnp.concatenate([both, dv_rows[rows, :]], 1)
        sums_ref[0:1, :] += jnp.sum(made, axis=0, keepdims=True)
        made = made.astype(BF16)
        gp_ref[rows, :] = made
        pulled = dot_nn(made, wt_ref[: 3 * g, :]) + dot_nn(gup_ref[rows, :], wt_ref[3 * g :, :])
        pulled = pulled.astype(BF16)
        for n in range(count):
            e_ref[step * count + n, 0] = pulled[n * unit : (n + 1) * unit]
        return carry

    lax.fori_loop(0, length // group, finish, 0)


def hidden_kernel(group, first, last, token_ref, gathered_ref, *refs):
    back_ref, slope_ref, act_ref, attb_ref, scaled_ref = refs[:5]
    at = 5
    if not first:
        old_back, old_up, old_sums = refs[at : at + 3]
        at += 3
    if last:
        raw_ref, norms_ref = refs[at : at + 2]
        at += 2
    if last:
        gup_ref, ga_ref, new_back, new_up, new_sums, vectors_ref, g_ref = refs[at:]
    else:
        gup_ref, ga_ref, new_back, new_up, new_sums, g_ref = refs[at:]
    length, width = g_ref.shape
    g = ga_ref.shape[1]
    unit = gathered_ref.shape[2]
    for n in range(gathered_ref.shape[0]):
        g_ref[n * unit : (n + 1) * unit, :] = gathered_ref[n, 0]
    new_sums[...] = jnp.zeros_like(new_sums) if first else old_sums[...]

    def pull(step, carry):
        rows = pl.ds(pl.multiple_of(step * group, group), group)
        made = dot_nn(g_ref[rows, :], back_ref[...])
        ga_ref[rows, :] = made[:, :g]
        grad_up = made[:, g:] * slope_ref[rows, :].astype(F32)
        new_sums[0:1, :] += jnp.sum(grad_up, axis=0, keepdims=True)
        gup_ref[rows, :] = grad_up.astype(BF16)
        return carry

    lax.fori_loop(0, length // group, pull, 0)

    tile = 256
    if last:
        start = raw_ref.shape[1] - gup_ref.shape[1]
        turned = norms_ref[...].astype(F32).T
    for column in range(0, width, tile):
        there = slice(column, column + tile)
        up = dot_tn(scaled_ref[:, there], gup_ref[...])
        if not first:
            up = up + old_up[there, :]
        if last:
            raw = raw_ref[there, start:].astype(F32)
            made = owner_part(
                up, raw, new_sums[0:1, :], turned[there, 2:3], turned[there, 3:4], there,
                vectors_ref,
            )
            owner_rows(made, column, new_up)
        else:
            new_up[there, :] = up
    both = jnp.concatenate([attb_ref[...], act_ref[...]], 1)
    if last:
        owners, cut = new_back.shape[0], new_back.shape[2]
    for row in range(0, both.shape[1], 128):
        here = slice(row, min(row + 128, both.shape[1]))
        part = dot_tn(both[:, here], g_ref[...])
        if not first:
            part = part + old_back[here, :]
        if last:
            for n in range(owners):
                new_back[n, here, :] = part[:, n * cut : (n + 1) * cut].astype(BF16)
        else:
            new_back[here, :] = part


def owner_rows(made, row, grad_ref):
    rows = grad_ref.shape[1]
    count = min(rows, made.shape[0])
    for at in range(0, made.shape[0], count):
        owner, inner = (row + at) // rows, (row + at) % rows
        grad_ref[owner, inner : inner + count, :] = made[at : at + count]


def owner_part(part, raw, sums, gain, shift, there, vectors_ref):
    made = (gain * part + shift * sums).astype(BF16)
    along = jnp.sum(raw * part, axis=1, keepdims=True)
    flat = jnp.sum(raw * sums, axis=1, keepdims=True)
    lane = lax.broadcasted_iota(jnp.int32, (part.shape[0], 128), 1)
    both = jnp.where(lane == 0, along, jnp.where(lane == 1, flat, 0.0))
    vectors_ref[:, there] = both.T[0:8, :]
    return made


def project_kernel(
    sequences, token_ref, raw_ref, norms_ref, *refs
):
    scaled_refs, gp_refs, sum_refs = [refs[n * sequences : (n + 1) * sequences] for n in range(3)]
    grad_ref, vectors_ref, sums_ref = refs[3 * sequences :]
    width, cols = raw_ref.shape[0], grad_ref.shape[2]
    sums_ref[...] = sum(ref[...] for ref in sum_refs)
    turned = norms_ref[...].astype(F32).T
    tile = 256
    for column in range(0, width, tile):
        there = slice(column, column + tile)
        part = sum(dot_tn(s[:, there], gp[...]) for s, gp in zip(scaled_refs, gp_refs))
        made = owner_part(
            part, raw_ref[there, :cols].astype(F32), sums_ref[0:1, :], turned[there, 0:1],
            turned[there, 1:2], there, vectors_ref,
        )
        owner_rows(made, column, grad_ref)


def fold_kernel(cols, pieces, place_ref, *refs):
    in_refs, back_refs = refs[:pieces], refs[pieces : 2 * pieces]
    norms_ref, extra_ref, raw_ref, w_out, wt_out, bias_out, back_out, backt_out = refs[2 * pieces :]
    rows, part = in_refs[0].shape[1], back_refs[0].shape[2]
    at = 0
    for in_ref, back_ref in zip(in_refs, back_refs):
        for n in range(in_ref.shape[0]):
            to = pl.multiple_of(place_ref[0, at] * rows, rows)
            raw_ref[pl.ds(to, rows), :] = in_ref[n]
            to = pl.multiple_of(place_ref[1, at] * part, part)
            backt_out[pl.ds(to, part), :] = back_ref[n].T
            at += 1
    turned = norms_ref[...].astype(F32).T
    w_out[:, :cols] = (raw_ref[:, :cols].astype(F32) * turned[:, 0:1]).astype(BF16)
    w_out[:, cols:] = (raw_ref[:, cols:].astype(F32) * turned[:, 2:3]).astype(BF16)
    wt_out[...] = w_out[...].T
    back_out[...] = backt_out[...].T
    made = dot_nn(norms_ref[...], raw_ref[...])
    bias_out[:, :cols] = made[1:2, :cols] + extra_ref[:, :cols].astype(F32)
    bias_out[:, cols:] = made[3:4, cols:] + extra_ref[:, cols:].astype(F32)


def kernel_call(body, outs, scratch, flops, args, scalars=1, own_specs=None, alias=None):
    specs = [pl.BlockSpec(memory_space=pltpu.SMEM)] * scalars + [
        pl.BlockSpec(memory_space=pltpu.VMEM) for _ in (*args[scalars:], *outs)
    ]
    for at, spec in (own_specs or {}).items():
        specs[at] = spec
    size = sum(math.prod(a.shape) * a.dtype.itemsize for a in list(args) + list(outs))
    return pl.pallas_call(
        body,
        grid=(1,) if own_specs else (),
        out_shape=tuple(outs),
        in_specs=specs[: len(args)],
        out_specs=tuple(specs[len(args) :]),
        scratch_shapes=scratch,
        input_output_aliases=alias or {},
        compiler_params=pltpu.CompilerParams(vmem_limit_bytes=VMEM_LIMIT),
        cost_estimate=pl.CostEstimate(
            flops=int(flops) // COST, bytes_accessed=int(size) // COST, transcendentals=0
        ),
    )(*args)


def shaped(*shape, dtype=BF16):
    return jax.ShapeDtypeStruct(shape, dtype)


def rotary_tables(length):
    half = ROTARY // 2
    freqs = 10000.0 ** (-np.arange(half, dtype=np.float64) * 2.0 / ROTARY)
    angles = np.arange(length)[:, None] * freqs[None, :]
    cosine, sine = np.cos(angles), np.sin(angles)
    none = np.zeros_like(sine)
    rest = np.zeros((length, HEAD_DIM - ROTARY))
    cos_head = np.concatenate([cosine, cosine, rest + 1.0], 1)
    first = np.concatenate([-sine, none, rest], 1)
    second = np.concatenate([none, sine, rest], 1)
    return tuple(
        jnp.asarray(np.concatenate([t, t], 1).astype(np.float32)) for t in (cos_head, first, second)
    )


def split_heads(values, heads, back=False):
    lead = values.shape[:-1]
    shape = (3, heads, HEAD_DIM) if back else (heads, 3, HEAD_DIM)
    return jnp.swapaxes(values.reshape(lead + shape), -3, -2).reshape(values.shape)


def local(
    dp,
    seq,
    inputs,
    w_qkv,
    b_qkv,
    w_out,
    b_out,
    w_up,
    b_up,
    w_down,
    b_down,
    norm1_gain,
    norm1_shift,
    norm2_gain,
    norm2_shift,
    cotangent,
):
    span, count, width = inputs.shape
    length = span * seq
    qkv_cols = w_qkv.shape[1]
    heads = qkv_cols // (3 * HEAD_DIM)
    g = heads * HEAD_DIM
    me = lax.axis_index("seq")
    token = jnp.zeros((8,), jnp.int32)
    tables = rotary_tables(length)

    sources = jnp.swapaxes(inputs, 0, 1)
    vectors = (norm1_gain, norm1_shift, norm2_gain, norm2_shift, b_out, b_down, b_qkv, b_up)
    blocks, vectors, sources = tie((w_qkv, w_up, w_out, w_down), vectors, sources)
    norms = jnp.stack(vectors[:6])
    small = jnp.concatenate([norms.reshape(-1), *vectors[6:]])
    dp_bits = list(range(dp.bit_length() - 1))
    seq_bits = list(range(seq.bit_length() - 1))
    gathered_x = lax.all_gather(sources, "seq", axis=0)
    in_block = jnp.concatenate([split_heads(blocks[0], heads), blocks[1]], 1)
    out_block = jnp.concatenate(blocks[2:], 0)
    small = small[None]
    for bit in dp_bits:
        small = cube_step(small, "dp", dp, bit)
    small, late = tie(small, cotangent)
    grads = jnp.swapaxes(late, 0, 1)
    gathered = lax.all_gather(grads, "seq", axis=0)
    in_pieces, out_pieces = [in_block[None]], [out_block[None]]
    for bit, back in zip(dp_bits, dp_bits[::-1]):
        in_pieces = cube(in_pieces, "dp", dp, bit)
        out_pieces = cube(out_pieces, "dp", dp, back)
    in_masks, out_masks = cube_masks(dp_bits), cube_masks(dp_bits[::-1])
    size = norms.size
    norms = small[:, :size][None]
    norms = cube_step(norms, "seq", seq, seq_bits[0])
    place = jnp.asarray([in_masks, out_masks], jnp.int32) ^ lax.axis_index("dp")
    at = 6 * norm1_gain.size
    qkv_bias = split_heads(small[:, at : at + b_qkv.size].reshape(-1), heads)
    up_bias = small[:, at + b_qkv.size :].reshape(-1)
    in_cols, back_rows = in_block.shape[1], out_block.shape[0]
    hidden = in_cols - qkv_cols
    for bit in seq_bits[1:]:
        norms = cube_step(norms, "seq", seq, bit)
    norms = norms.reshape(seq, dp, 6, -1).transpose(2, 1, 0, 3).reshape(6, width)
    out_bias, down_bias = norms[4].astype(F32), norms[5].astype(F32)
    norms = jnp.concatenate([norms, jnp.zeros((2, width), BF16)], 0)
    raw, folded, folded_t, bias, w_back, back_t = kernel_call(
        functools.partial(fold_kernel, qkv_cols, len(in_pieces)),
        [
            shaped(width, in_cols),
            shaped(width, in_cols),
            shaped(in_cols, width),
            shaped(1, in_cols, dtype=F32),
            shaped(back_rows, width),
            shaped(width, back_rows),
        ],
        [],
        1e7,
        (
            place,
            *in_pieces,
            *out_pieces,
            norms,
            jnp.concatenate([qkv_bias, up_bias])[None],
        ),
    )

    unit = span
    group = math.gcd(length, 256)
    block = math.gcd(length, 256)
    matmul = 2.0 * length * width
    pairs = 2.0 * heads * length * length * 64

    def of_sequence(s):
        return pl.BlockSpec((seq, 1, unit, width), lambda i: (0, s, 0, 0))

    def call_held(body, outs, scratch, flops, args, s, place, held, more=()):
        args = (*args, *held)
        own = {at: of_sequence(s) for at in (len(args) + place, *more)}
        if held:
            own[len(args) - 1] = pl.BlockSpec(memory_space=pl.ANY)
        return kernel_call(
            body, outs, scratch, flops, args, own_specs=own,
            alias={len(args) - 1: place} if held else None,
        )

    def run_forward(token, s, *held):
        return call_held(
            functools.partial(forward_kernel, heads, group, block, len(held)),
            [
                shaped(length, width),
                shaped(length, hidden),
                shaped(length, hidden),
                shaped(length, g),
                shaped(length, g),
                shaped(length, g),
                shaped(g, length, dtype=F32),
                shaped(heads, length, dtype=F32),
                shaped(length, g),
                shaped(seq, count, unit, width),
            ],
            [],
            matmul * (4 * g + 2 * hidden) + 8 * pairs,
            (token, gathered_x, folded, bias, *tables, w_back),
            s,
            9,
            held,
            (1,),
        )

    def run_hidden(token, s, gathered, f, old, last):
        cut = width // dp
        if last:
            wide = [
                shaped(dp, back_rows, cut),
                shaped(dp, cut, hidden),
                shaped(8, hidden, dtype=F32),
                shaped(8, width, dtype=F32),
            ]
        else:
            wide = [
                shaped(back_rows, width, dtype=F32),
                shaped(width, hidden, dtype=F32),
                shaped(8, hidden, dtype=F32),
            ]
        return kernel_call(
            functools.partial(hidden_kernel, group, not old, last),
            [shaped(length, hidden), shaped(length, g, dtype=F32)] + wide,
            [pltpu.VMEM((length, width), BF16)],
            matmul * (2 * g + 3 * hidden),
            (token, gathered, back_t, f[2], f[1], f[8], f[0], *old)
            + ((raw, norms) if last else ()),
            own_specs={1: of_sequence(s)},
        )

    def run_backward(token, s, f, made, *held):
        return call_held(
            functools.partial(backward_kernel, heads, group, unit, block, len(held)),
            [
                shaped(length, 3 * g),
                shaped(8, 3 * g, dtype=F32),
                shaped(seq, count, unit, width),
            ],
            [pltpu.VMEM((length, g), F32) for _ in range(3)],
            matmul * (3 * g + hidden) + 16 * pairs,
            (token, made[1], folded_t, *tables, *f[3:8], made[0]),
            s,
            2,
            held,
        )

    f0 = run_forward(token, 0)
    f1 = run_forward(token, 1, f0[9])
    branches = lax.psum_scatter(f1[9], "seq", scatter_dimension=0)
    (sources, grads), f1_lse = tie((sources, grads), f1[7])
    f1 = (*f1[:7], f1_lse, *f1[8:])
    late_sums = sum(jnp.sum(grad.astype(F32), 0) for grad in grads)
    h0 = run_hidden(token, 0, gathered, f0, (), False)
    b0 = run_backward(token, 0, f0, h0)
    token, b0_sums = tie(token, b0[1])
    h1 = run_hidden(token, 1, gathered, f1, h0[2:5], True)
    early = [CubeSum(h1[2], "dp", dp_bits[::-1]), CubeSum(h1[3], "dp", dp_bits)]
    token, sent = tie(token, [blocks.ready() for blocks in early])
    for blocks, value in zip(early, sent):
        blocks.send(value)
    b1 = run_backward(token, 1, f1, h1, b0[2])
    token, b1, gots = tie(token, b1, [blocks.got for blocks in early])
    for blocks, got in zip(early, gots):
        blocks.got = got
        blocks.land()
    b1_sums = b1[1]
    e = lax.psum_scatter(b1[2], "seq", scatter_dimension=0)
    grad_qkv, norm_one, qkv_sums = kernel_call(
        functools.partial(project_kernel, count),
        [
            shaped(dp, width // dp, qkv_cols),
            shaped(8, width, dtype=F32),
            shaped(8, qkv_cols, dtype=F32),
        ],
        [],
        matmul * 3 * g * count,
        (token, raw, norms, f0[0], f1[0], b0[0], b1[0], b0_sums, b1_sums),
    )
    last_qkv = CubeSum(grad_qkv, "dp", dp_bits)
    last_qkv.send(last_qkv.ready())
    last_qkv.land()
    qkv_sums = qkv_sums[0]
    rows = width // dp
    vectors = jnp.concatenate([norm_one[:2], h1[5][:2], late_sums[None]], 0)
    vectors = vectors.reshape(5, dp, seq, -1).transpose(1, 2, 0, 3).reshape(dp, -1)
    cut = vectors.shape[1]
    biases = [split_heads(qkv_sums, heads, back=True).reshape(dp, -1), h1[4][0].reshape(dp, -1)]
    vectors = jnp.concatenate([vectors] + biases, 1)
    summed = cube_sum(vectors, "dp", dp_bits)
    grad_b_qkv, grad_b_up = summed[cut : cut + b_qkv.size], summed[cut + b_qkv.size :]
    summed, branches = tie(summed, branches)
    last = CubeSum(summed[:cut].reshape(seq, 5, -1), "seq", seq_bits)
    norms_out = last.finish()
    output = jnp.stack(
        [
            (sources[s].astype(F32) + branches[s].astype(F32) + (out_bias + down_bias)[None])
            .astype(BF16)
            for s in range(count)
        ],
        1,
    )
    output, norms_out, pulled = tie(output, norms_out, e)

    done = early[0].finish()
    grad_w_out, grad_w_down = done[:g], done[g:]
    grad_w_up = early[1].finish()
    grad_w_qkv = last_qkv.finish()
    grad_w_qkv = split_heads(grad_w_qkv, heads, back=True)

    grads_in = []
    for s in range(count):
        source = sources[s].astype(F32)
        mean = jnp.mean(source, 1, keepdims=True)
        centred = source - mean
        inverse = lax.rsqrt(jnp.mean(centred * centred, 1, keepdims=True) + EPSILON)
        scaled = centred * inverse
        e = pulled[s].astype(F32)
        middle = jnp.mean(e, 1, keepdims=True)
        along = jnp.mean(e * scaled, 1, keepdims=True)
        grads_in.append(
            (grads[s].astype(F32) + inverse * (e - middle - scaled * along)).astype(BF16)
        )
    return (
        output,
        jnp.stack(grads_in, 1),
        grad_w_qkv,
        grad_b_qkv,
        grad_w_out,
        norms_out[4],
        grad_w_up,
        grad_b_up,
        grad_w_down,
        norms_out[4],
        norms_out[0],
        norms_out[1],
        norms_out[2],
        norms_out[3],
    )


def solution(mesh):
    tokens = P("seq", "dp", None)
    rows, columns = P("dp", "seq"), P("seq", "dp")
    wide, flat = P(("seq", "dp")), P(("dp", "seq"))
    return jax.shard_map(
        functools.partial(local, mesh.shape["dp"], mesh.shape["seq"]),
        mesh=mesh,
        in_specs=(
            tokens, rows, wide, columns, flat, rows, wide, columns, flat, flat, flat, flat, flat,
            tokens,
        ),
        out_specs=(
            tokens, tokens, rows, wide, columns, flat, rows, wide, columns, flat, flat, flat,
            flat, flat,
        ),
        check_vma=False,
    )
```
